32 devices in a mesh: parts: 2 (over y), row: 4 (over z), col: 4 (over x, core).
Axes of the slice: x: 2, y: 2, z: 4, core: 2. Of those that a mesh axis runs over, the one named last changes fastest.
Arguments:
- features: bfloat16 [8192, 128], P(('parts', 'col', 'row')), parts along dimension 0, may hold values from -6 to 6
- block_values: bfloat16 [4096, 128, 128], P(('parts', 'row', 'col')), parts along dimension 0, may hold values from -0.25 to 0.25
- block_rows: int32 [4096], P(('parts', 'row', 'col')), parts along dimension 0, may hold values from 0 to 7
- block_cols: int32 [4096], P(('parts', 'row', 'col')), parts along dimension 0, may hold values from 0 to 7
- block_count: int32 [32], P(('parts', 'row', 'col')), parts along dimension 0, may hold values from 32 to 128, as said below
- weight: bfloat16 [128, 256], replicated, may hold values from -0.5 to 0.5
- bias: float32 [256], replicated, may hold values from -3 to 3
- cotangent: bfloat16 [8192, 256], P(('parts', 'row', 'col')), parts along dimension 0, may hold values from -6 to 6
Outputs:
- hidden: bfloat16 [8192, 256], P(('parts', 'row', 'col')), parts along dimension 0
- grad_weight: float32 [256, 256], P('parts'), parts along dimension 0
- grad_bias: float32 [512], P('parts'), parts along dimension 0
- grad_features: bfloat16 [8192, 128], P(('parts', 'col', 'row')), parts along dimension 0
The draws below stay inside these ranges and needn't reach their ends.
There are 2 independent parts, one for each index of `parts`. The reference program is written for one: setup_inputs(seed, part) draws one part's arguments, and reference() takes and returns one part's arrays. A program takes and returns all parts, laid end to end along the dimension named above; an argument that names none is the same for every part. Nothing has to cross between parts.
Inputs may be any that keep to these rules, and one draw needn't show every extreme that they name: `block_count`: slot j of a device is live when j is below the device's count; some device of every partition has 128 live slots.
All inputs are finite; a program needn't handle non-finite values.
Results may differ from the reference program's by a relative error of at most 0.02.
Values may be sent and summed in bfloat16 or wider, within the bound.
No kernel may reach another device: no remote copies, remote signals or barrier semaphores. Data moves between devices by JAX's collectives and lax.ppermute only.
A program may use at most 64 MiB of HBM per device.

```python
import jax
import jax.numpy as jnp
from jax import lax

F_IN = 128
HID = 256
BS = 128
CAP = 128
COL_GROUPS = 4
DEVS = 16
NODES = 4096
SLOTS = 2048
ROW_BLOCKS = 8
COL_BLOCKS = 8


def draw_block_count(key, part):
    key = jax.random.fold_in(key, 7)
    key_counts, key_full = jax.random.split(key)
    counts_drawn = jax.random.randint(key_counts, (DEVS,), max(1, CAP // 4), CAP + 1)
    full_device = jax.random.randint(key_full, (), 0, DEVS)
    return jnp.where(jnp.arange(DEVS) == full_device, CAP, counts_drawn).astype(jnp.int32)


def place_ends(result, rng, least, largest):
    longest = result.shape.index(max(result.shape))
    spots = []
    for shift in (0, 1):
        where = [jax.random.randint(jax.random.fold_in(rng, axis), (), 0, length) for axis, length in enumerate(result.shape)]
        where[longest] = (where[longest] + shift) % result.shape[longest]
        spots.append(tuple(where))
    return result.at[spots[0]].set(least).at[spots[1]].set(largest)


def levels(own_key, shape, pieces, low, largest):
    def one(axis_at, parts):
        draws = jax.random.uniform(jax.random.fold_in(jax.random.fold_in(own_key, 6), axis_at), (parts,), jnp.float32, low / len(pieces), largest / len(pieces))
        return jnp.repeat(jnp.exp(draws), shape[axis_at] // parts).reshape((-1,) + (1,) * (len(shape) - axis_at - 1))

    factor_of = one(*pieces[0])
    for cut in pieces[1:]:
        factor_of = factor_of * one(*cut)
    return factor_of


def noise(stream_key, extent, width, limit, cuts=(), kind=jnp.bfloat16):
    gain = levels(stream_key, extent, cuts, -0.22, 0.18) if cuts else 1.0
    entries = jax.random.normal(stream_key, extent, jnp.float32) * width * gain
    return jnp.minimum(jnp.maximum(entries, -limit), limit).astype(kind)


def setup_inputs(seed: int = 0, part: int = 0) -> dict:
    splits = jax.random.split(jax.random.key(seed), 9)
    own_keys = jax.random.split(jax.random.fold_in(splits[8], part), 9)
    return {
        "features": noise(own_keys[0], (NODES, F_IN), 1.0, 6.0, ((0, 16),)),
        "block_values": noise(own_keys[1], (SLOTS, BS, BS), (4 * BS) ** -0.5, 0.25, ((0, 16),)),
        "block_rows": place_ends(jax.random.randint(own_keys[2], (SLOTS,), 0, ROW_BLOCKS), jax.random.fold_in(own_keys[2], 1), 0, ROW_BLOCKS - 1).astype(jnp.int32),
        "block_cols": place_ends(jax.random.randint(own_keys[3], (SLOTS,), 0, COL_BLOCKS), jax.random.fold_in(own_keys[3], 1), 0, COL_BLOCKS - 1).astype(jnp.int32),
        "block_count": draw_block_count(jax.random.fold_in(jax.random.fold_in(splits[8], part), 71), part),
        "weight": noise(splits[5], (F_IN, HID), F_IN ** -0.5, 0.5),
        "bias": noise(splits[6], (HID,), 0.5, 3.0, (), jnp.float32),
        "cotangent": noise(own_keys[7], (NODES, HID), 1.0, 6.0, ((0, 16),)),
    }


def spread(per_device, source_blocks, block_total, forward_pass):
    def step_fn(summed, device_item):
        values, rows_here, cols_here, live_here = device_item
        values = values.astype(jnp.float32)
        if forward_pass:
            chosen = source_blocks[cols_here].astype(jnp.float32) * live_here[:, None, None]
            products = jnp.einsum("spq,sqf->spf", values, chosen)
            summed = summed.at[rows_here].add(products)
        else:
            chosen = source_blocks[rows_here].astype(jnp.float32) * live_here[:, None, None]
            products = jnp.einsum("spq,spf->sqf", values, chosen)
            summed = summed.at[cols_here].add(products)
        return summed, None

    initial = jnp.zeros((block_total, BS, source_blocks.shape[2]), jnp.float32)
    return lax.scan(step_fn, initial, per_device)[0]


def reference(features, block_values, block_rows, block_cols, block_count, weight, bias, cotangent):
    slot_total = block_values.shape[0]
    slot_ids = jnp.arange(slot_total, dtype=jnp.int32)
    slot_owner = (slot_ids // CAP).astype(jnp.int32)
    live_mask = ((slot_ids % CAP) < block_count[slot_owner]).astype(jnp.float32)
    row_global = ((slot_owner // COL_GROUPS) * ROW_BLOCKS + block_rows).astype(jnp.int32)
    col_global = ((slot_owner % COL_GROUPS) * COL_BLOCKS + block_cols).astype(jnp.int32)
    block_total = NODES // BS
    per_device = (block_values.reshape(DEVS, CAP, BS, BS), row_global.reshape(DEVS, CAP),
                  col_global.reshape(DEVS, CAP), live_mask.reshape(DEVS, CAP))
    summed = spread(per_device, features.reshape(block_total, BS, F_IN), block_total, True)
    aggregate = summed.reshape(NODES, F_IN).astype(jnp.bfloat16)
    pre_act = jnp.dot(aggregate, weight, preferred_element_type=jnp.float32) + bias
    sigmoid_pre = jax.nn.sigmoid(pre_act)
    hidden = (pre_act * sigmoid_pre).astype(jnp.bfloat16)
    pre_grad = (cotangent.astype(jnp.float32) * sigmoid_pre * (1.0 + pre_act * (1.0 - sigmoid_pre))).astype(jnp.bfloat16)
    norm_scale = float(NODES) ** -0.5
    grad_weight = jnp.dot(aggregate.T, pre_grad, preferred_element_type=jnp.float32) * norm_scale
    grad_bias = jnp.sum(pre_grad.astype(jnp.float32), axis=0) * norm_scale
    agg_grad = jnp.dot(pre_grad, weight.T, preferred_element_type=jnp.float32).astype(jnp.bfloat16)
    summed_back = spread(per_device, agg_grad.reshape(block_total, BS, F_IN), block_total, False)
    grad_features = summed_back.reshape(NODES, F_IN).astype(jnp.bfloat16)
    return hidden, grad_weight, grad_bias, grad_features
```

```python
import functools

import jax
import jax.numpy as jnp
from jax import lax
from jax.experimental import pallas as pl
from jax.experimental.pallas import tpu as pltpu
from jax.sharding import PartitionSpec as P

F32 = jnp.float32
BF16 = jnp.bfloat16
ROWS = 4
COLS = 4
WHOLE = pl.BlockSpec(memory_space=pltpu.VMEM)
SCALARS = pl.BlockSpec(memory_space=pltpu.SMEM)


def pick_rows(pick_index, live_mask, source_rows):
    source_count = source_rows.shape[0]
    onehot = (
        (pick_index[:, None] == jnp.arange(source_count, dtype=jnp.int32)[None, :])
        & live_mask[:, None]
    ).astype(jnp.bfloat16)
    chosen = jnp.dot(
        onehot, source_rows.reshape(source_count, -1), preferred_element_type=jnp.float32
    ).astype(jnp.bfloat16)
    return chosen.reshape((pick_index.shape[0],) + source_rows.shape[1:])


def slot_terms(values, pick_index, live_mask, source_rows, forward_pass):
    chosen = pick_rows(pick_index, live_mask, source_rows)
    if forward_pass:
        return jnp.einsum("spq,sqf->spf", values, chosen, preferred_element_type=jnp.float32)
    return jnp.einsum("spq,spf->sqf", values, chosen, preferred_element_type=jnp.float32)


def place_terms(products, place_index, blocks):
    block_ids = jnp.arange(blocks, dtype=jnp.int32)
    onehot = (block_ids[:, None] == place_index[None, :]).astype(jnp.bfloat16)
    flat = products.reshape(products.shape[0], -1)
    upper = flat.astype(jnp.bfloat16)
    lower = (flat - upper.astype(jnp.float32)).astype(jnp.bfloat16)
    placed = jnp.dot(onehot, upper, preferred_element_type=jnp.float32)
    placed = placed + jnp.dot(onehot, lower, preferred_element_type=jnp.float32)
    return placed.reshape(blocks * products.shape[1], products.shape[2])


def by_slots(features, block_values, block_rows, block_cols, block_count, weight, bias, cotangent):
    block_size = block_values.shape[1]
    slot_total = block_values.shape[0]
    live_mask = jnp.arange(slot_total, dtype=jnp.int32) < block_count[0]
    node_rows = cotangent.shape[0]
    width_in = features.shape[1]
    column_rows = lax.all_gather(features, "row", axis=0, tiled=True)
    column_blocks = column_rows.reshape(-1, block_size, width_in)
    forward_terms = slot_terms(block_values, block_cols, live_mask, column_blocks, True)
    aggregate = lax.psum_scatter(
        place_terms(
            forward_terms, block_rows, lax.axis_size("col") * node_rows // block_size
        ).astype(jnp.bfloat16),
        "col",
        scatter_dimension=0,
        tiled=True,
    ).astype(jnp.float32)
    aggregate = aggregate.astype(jnp.bfloat16)
    pre_act = jnp.dot(aggregate, weight, preferred_element_type=jnp.float32) + bias
    sigmoid_pre = jax.nn.sigmoid(pre_act)
    hidden = (pre_act * sigmoid_pre).astype(jnp.bfloat16)
    pre_grad = (
        cotangent.astype(jnp.float32) * sigmoid_pre * (1.0 + pre_act * (1.0 - sigmoid_pre))
    ).astype(jnp.bfloat16)
    grad_local = lax.dot_general(
        aggregate, pre_grad, (((0,), (0,)), ((), ())), preferred_element_type=jnp.float32
    )
    bias_local = jnp.sum(pre_grad.astype(jnp.float32), axis=0)
    grad_weight, grad_bias = lax.psum((grad_local, bias_local), ("row", "col"))
    norm_scale = float(node_rows * lax.axis_size("row") * lax.axis_size("col")) ** (-0.5)
    agg_grad = lax.dot_general(
        pre_grad, weight, (((1,), (1,)), ((), ())), preferred_element_type=jnp.float32
    ).astype(jnp.bfloat16)
    stripe_rows = lax.all_gather(agg_grad, "col", axis=0, tiled=True)
    stripe_blocks = stripe_rows.reshape(-1, block_size, width_in)
    backward_terms = slot_terms(block_values, block_rows, live_mask, stripe_blocks, False)
    grad_features = lax.psum_scatter(
        place_terms(
            backward_terms, block_cols, lax.axis_size("row") * node_rows // block_size
        ).astype(jnp.bfloat16),
        "row",
        scatter_dimension=0,
        tiled=True,
    )
    return (hidden, grad_weight * norm_scale, grad_bias * norm_scale, grad_features)


def densify_kernel(chunk, row_blocks, col_blocks, rows_ref, cols_ref, count_ref, values_ref, tile_ref, acc):
    step = pl.program_id(0)
    block = values_ref.shape[1]

    @pl.when(step == 0)
    def _():
        acc[...] = jnp.zeros_like(acc)

    first = step * chunk

    def add_slot(i, carry):
        place = rows_ref[first + i] * col_blocks + cols_ref[first + i]
        acc[place] = acc[place] + values_ref[i].astype(F32)
        return carry

    lax.fori_loop(0, jnp.clip(count_ref[0] - first, 0, chunk), add_slot, 0)

    @pl.when(step == pl.num_programs(0) - 1)
    def _():
        for r in range(row_blocks):
            for c in range(col_blocks):
                tile_ref[pl.ds(r * block, block), pl.ds(c * block, block)] = acc[
                    r * col_blocks + c
                ].astype(BF16)


def densify(values, rows, cols, count, row_blocks, col_blocks):
    slots, block, _ = values.shape
    chunk = 16
    return pl.pallas_call(
        functools.partial(densify_kernel, chunk, row_blocks, col_blocks),
        grid=(slots // chunk,),
        in_specs=[SCALARS] * 3
        + [pl.BlockSpec((chunk, block, block), lambda i: (i, 0, 0))],
        out_specs=pl.BlockSpec((row_blocks * block, col_blocks * block), lambda i: (0, 0)),
        out_shape=jax.ShapeDtypeStruct((row_blocks * block, col_blocks * block), BF16),
        scratch_shapes=[pltpu.VMEM((row_blocks * col_blocks, block, block), F32)],
        cost_estimate=pl.CostEstimate(flops=slots * block * block, bytes_accessed=values.size * 2, transcendentals=0),
        name="densify",
    )(rows, cols, count, values)


def forward_kernel(tile_ref, x0, x1, x2, x3, send_ref, keep_ref):
    row = lax.axis_index("row")
    core = lax.rem(lax.axis_index("col"), 2)
    rows = x0.shape[0]

    def part(block):
        total = None
        for k, x in enumerate((x0, x1, x2, x3)):
            col_at = pl.multiple_of(jnp.bitwise_xor(row, k) * rows, rows)
            tile = tile_ref[pl.ds(pl.multiple_of(block * rows, rows), rows), pl.ds(col_at, rows)]
            term = jnp.dot(tile, x[...], preferred_element_type=F32)
            total = term if total is None else total + term
        return total

    for x in range(2):
        send_ref[pl.ds(x * rows, rows), :] = part(2 * x + 1 - core).astype(BF16)
    for x in range(2):
        keep_ref[pl.ds(x * rows, rows), :] = part(2 * x + core)


def layer_kernel(keep_ref, sib_ref, far_ref, cot_ref, cot_far_ref, weight_ref, bias_ref,
                 hidden_ref, grad_ref, gw_ref, gb_ref):
    mine = lax.rem(lax.axis_index("col") // 2, 2)
    rows = cot_ref.shape[0]
    weight = weight_ref[...]
    gw = None
    gb = None
    for other in range(2):
        where = pl.multiple_of(jnp.bitwise_xor(mine, other) * rows, rows)
        block = pl.ds(where, rows)
        aggregate = (
            keep_ref[block, :] + sib_ref[block, :].astype(F32) + far_ref[block, :].astype(F32)
        ).astype(BF16)
        pre_act = jnp.dot(aggregate, weight, preferred_element_type=F32) + bias_ref[...]
        sigmoid_pre = jax.nn.sigmoid(pre_act)
        if other == 0:
            hidden_ref[...] = (pre_act * sigmoid_pre).astype(BF16)
        cot = (cot_far_ref if other else cot_ref)[...].astype(F32)
        pre_grad = (cot * sigmoid_pre * (1.0 + pre_act * (1.0 - sigmoid_pre))).astype(BF16)
        grad_ref[block, :] = lax.dot_general(
            pre_grad, weight, (((1,), (1,)), ((), ())), preferred_element_type=F32
        ).astype(BF16)
        term = lax.dot_general(
            aggregate, pre_grad, (((0,), (0,)), ((), ())), preferred_element_type=F32
        )
        bias_term = jnp.sum(pre_grad.astype(F32), axis=0, keepdims=True)
        gw = term if gw is None else gw + term
        gb = bias_term if gb is None else gb + bias_term
    gw_ref[...] = gw
    gb_ref[...] = gb


def backward_kernel(tile_ref, own_ref, sib_ref, keep_ref, send1, send2, send3):
    row = lax.axis_index("row")
    core = lax.rem(lax.axis_index("col"), 2)
    rows = keep_ref.shape[0]
    for k, out in ((1, send1), (2, send2), (3, send3), (0, keep_ref)):
        col_at = pl.multiple_of(jnp.bitwise_xor(row, k) * rows, rows)
        total = None
        for half, ref in ((core, own_ref), (1 - core, sib_ref)):
            for x in range(2):
                row_at = pl.multiple_of((2 * x + half) * rows, rows)
                tile = tile_ref[pl.ds(row_at, rows), pl.ds(col_at, rows)]
                term = lax.dot_general(
                    tile, ref[pl.ds(x * rows, rows), :], (((0,), (0,)), ((), ())),
                    preferred_element_type=F32,
                )
                total = term if total is None else total + term
        out[...] = total.astype(out.dtype)


def swap(array, axis, bit):
    size = lax.axis_size(axis)
    return lax.ppermute(array, axis, [(i, i ^ bit) for i in range(size)])


def dense_tile(features, block_values, block_rows, block_cols, block_count, weight, bias, cotangent):
    block_size = block_values.shape[1]
    node_rows = cotangent.shape[0]
    width_in = features.shape[1]
    hid = cotangent.shape[1]
    row_blocks = COLS * node_rows // block_size
    col_blocks = ROWS * node_rows // block_size
    shards = [features] + [swap(features, "row", k) for k in (1, 2, 3)]
    cot_far = swap(cotangent, "col", 2)
    tile = densify(block_values, block_rows, block_cols, block_count, row_blocks, col_blocks)
    half = jax.ShapeDtypeStruct((2 * node_rows, width_in), BF16)
    send, keep = pl.pallas_call(
        forward_kernel,
        in_specs=[WHOLE] * 5,
        out_specs=[WHOLE] * 2,
        out_shape=[half, jax.ShapeDtypeStruct(half.shape, F32)],
        name="forward",
    )(tile, *shards)
    sib = swap(send, "col", 1)
    far = swap((keep + sib.astype(F32)).astype(BF16), "col", 2)
    hidden, agg_grad, gw, gb = pl.pallas_call(
        layer_kernel,
        in_specs=[WHOLE] * 7,
        out_specs=[WHOLE] * 4,
        out_shape=[
            jax.ShapeDtypeStruct((node_rows, hid), BF16),
            half,
            jax.ShapeDtypeStruct((width_in, hid), F32),
            jax.ShapeDtypeStruct((1, hid), F32),
        ],
        name="layer",
    )(keep, sib, far, cotangent, cot_far, weight, bias.reshape(1, hid))
    grad_sib = swap(agg_grad, "col", 1)
    block = jax.ShapeDtypeStruct((node_rows, width_in), BF16)
    own, *sends = pl.pallas_call(
        backward_kernel,
        in_specs=[WHOLE] * 3,
        out_specs=[WHOLE] * 4,
        out_shape=[jax.ShapeDtypeStruct(block.shape, F32)] + [block] * 3,
        name="backward",
    )(tile, agg_grad, grad_sib)
    got = [swap(part, "row", k) for k, part in zip((1, 2, 3), sends)]
    grad_features = (own + got[0].astype(F32) + got[1].astype(F32) + got[2].astype(F32)).astype(BF16)

    both = jnp.concatenate([gw, jnp.broadcast_to(gb, (16, hid))], axis=0).astype(BF16)
    both = both.astype(F32) + swap(both, "col", 1).astype(F32)
    mine = (lax.axis_index("col") // 2) % 2
    part_rows = width_in // 2
    part = lax.dynamic_slice_in_dim(both, mine * part_rows, part_rows, 0)
    part = jnp.concatenate([part, both[width_in:]], axis=0).astype(BF16)
    row = lax.axis_index("row")
    parts = jnp.stack([part] + [swap(part, "row", k) for k in (1, 2, 3)])
    total = None
    for j in range(ROWS):
        term = lax.dynamic_index_in_dim(parts, row ^ j, 0, keepdims=False).astype(F32)
        total = term if total is None else total + term
    total = total.astype(BF16)
    total_far = swap(total, "col", 2)
    first = jnp.where(mine == 0, total, total_far)
    second = jnp.where(mine == 0, total_far, total)
    norm_scale = float(node_rows * ROWS * COLS) ** (-0.5)
    grad_weight = jnp.concatenate([first[:part_rows], second[:part_rows]], axis=0).astype(F32) * norm_scale
    grad_bias = first[part_rows].astype(F32) * norm_scale
    return hidden, grad_weight, grad_bias, grad_features


def solution(mesh):
    in_specs = (
        P(("parts", "col", "row"), None),
        P(("parts", "row", "col"), None, None),
        P(("parts", "row", "col")),
        P(("parts", "row", "col")),
        P(("parts", "row", "col")),
        P(),
        P(),
        P(("parts", "row", "col"), None),
    )
    out_specs = (
        P(("parts", "row", "col"), None),
        P("parts", None),
        P("parts"),
        P(("parts", "col", "row"), None),
    )
    small = mesh.shape["row"] == ROWS and mesh.shape["col"] == COLS
    return jax.shard_map(
        dense_tile if small else by_slots,
        mesh=mesh,
        in_specs=in_specs,
        out_specs=out_specs,
        check_vma=False,
    )
```

```python
import functools

import jax
import jax.numpy as jnp
from jax import lax
from jax.experimental import pallas as pl
from jax.experimental.pallas import tpu as pltpu
from jax.sharding import PartitionSpec as P

F32 = jnp.float32
BF16 = jnp.bfloat16
ROWS = 4
COLS = 4
WHOLE = pl.BlockSpec(memory_space=pltpu.VMEM)
SCALARS = pl.BlockSpec(memory_space=pltpu.SMEM)
LIMIT = pltpu.CompilerParams(vmem_limit_bytes=16 * 2**20)
BIAS_ROWS = 16


def pick_rows(pick_index, live_mask, source_rows):
    source_count = source_rows.shape[0]
    onehot = (
        (pick_index[:, None] == jnp.arange(source_count, dtype=jnp.int32)[None, :])
        & live_mask[:, None]
    ).astype(jnp.bfloat16)
    chosen = jnp.dot(
        onehot, source_rows.reshape(source_count, -1), preferred_element_type=jnp.float32
    ).astype(jnp.bfloat16)
    return chosen.reshape((pick_index.shape[0],) + source_rows.shape[1:])


def slot_terms(values, pick_index, live_mask, source_rows, forward_pass):
    chosen = pick_rows(pick_index, live_mask, source_rows)
    if forward_pass:
        return jnp.einsum("spq,sqf->spf", values, chosen, preferred_element_type=jnp.float32)
    return jnp.einsum("spq,spf->sqf", values, chosen, preferred_element_type=jnp.float32)


def place_terms(products, place_index, blocks):
    block_ids = jnp.arange(blocks, dtype=jnp.int32)
    onehot = (block_ids[:, None] == place_index[None, :]).astype(jnp.bfloat16)
    flat = products.reshape(products.shape[0], -1)
    upper = flat.astype(jnp.bfloat16)
    lower = (flat - upper.astype(jnp.float32)).astype(jnp.bfloat16)
    placed = jnp.dot(onehot, upper, preferred_element_type=jnp.float32)
    placed = placed + jnp.dot(onehot, lower, preferred_element_type=jnp.float32)
    return placed.reshape(blocks * products.shape[1], products.shape[2])


def by_slots(features, block_values, block_rows, block_cols, block_count, weight, bias, cotangent):
    block_size = block_values.shape[1]
    slot_total = block_values.shape[0]
    live_mask = jnp.arange(slot_total, dtype=jnp.int32) < block_count[0]
    node_rows = cotangent.shape[0]
    width_in = features.shape[1]
    column_rows = lax.all_gather(features, "row", axis=0, tiled=True)
    column_blocks = column_rows.reshape(-1, block_size, width_in)
    forward_terms = slot_terms(block_values, block_cols, live_mask, column_blocks, True)
    aggregate = lax.psum_scatter(
        place_terms(
            forward_terms, block_rows, lax.axis_size("col") * node_rows // block_size
        ).astype(jnp.bfloat16),
        "col",
        scatter_dimension=0,
        tiled=True,
    ).astype(jnp.float32)
    aggregate = aggregate.astype(jnp.bfloat16)
    pre_act = jnp.dot(aggregate, weight, preferred_element_type=jnp.float32) + bias
    sigmoid_pre = jax.nn.sigmoid(pre_act)
    hidden = (pre_act * sigmoid_pre).astype(jnp.bfloat16)
    pre_grad = (
        cotangent.astype(jnp.float32) * sigmoid_pre * (1.0 + pre_act * (1.0 - sigmoid_pre))
    ).astype(jnp.bfloat16)
    grad_local = lax.dot_general(
        aggregate, pre_grad, (((0,), (0,)), ((), ())), preferred_element_type=jnp.float32
    )
    bias_local = jnp.sum(pre_grad.astype(jnp.float32), axis=0)
    grad_weight, grad_bias = lax.psum((grad_local, bias_local), ("row", "col"))
    norm_scale = float(node_rows * lax.axis_size("row") * lax.axis_size("col")) ** (-0.5)
    agg_grad = lax.dot_general(
        pre_grad, weight, (((1,), (1,)), ((), ())), preferred_element_type=jnp.float32
    ).astype(jnp.bfloat16)
    stripe_rows = lax.all_gather(agg_grad, "col", axis=0, tiled=True)
    stripe_blocks = stripe_rows.reshape(-1, block_size, width_in)
    backward_terms = slot_terms(block_values, block_rows, live_mask, stripe_blocks, False)
    grad_features = lax.psum_scatter(
        place_terms(
            backward_terms, block_cols, lax.axis_size("row") * node_rows // block_size
        ).astype(jnp.bfloat16),
        "row",
        scatter_dimension=0,
        tiled=True,
    )
    return (hidden, grad_weight * norm_scale, grad_bias * norm_scale, grad_features)


def densify_kernel(chunks, row_blocks, col_blocks, rows_ref, cols_ref, count_ref, values_ref, tile_ref, held, acc, sems):
    slots, block, _ = values_ref.shape
    size = slots // chunks
    copies = [
        pltpu.make_async_copy(
            values_ref.at[pl.ds(i * size, size)], held.at[pl.ds(i * size, size)], sems.at[i]
        )
        for i in range(chunks)
    ]
    for copy in copies:
        copy.start()
    acc[...] = jnp.zeros_like(acc)
    live = count_ref[0]

    def add_slot(i, carry):
        place = rows_ref[i] * col_blocks + cols_ref[i]
        acc[place] = acc[place] + held[i].astype(F32)
        return carry

    for i, copy in enumerate(copies):
        copy.wait()
        lax.fori_loop(i * size, jnp.clip(live, i * size, (i + 1) * size), add_slot, 0)
    for r in range(row_blocks):
        for c in range(col_blocks):
            tile_ref[pl.ds(r * block, block), pl.ds(c * block, block)] = acc[
                r * col_blocks + c
            ].astype(BF16)


def densify(values, rows, cols, count, row_blocks, col_blocks):
    slots, block, _ = values.shape
    chunks = 8
    return pl.pallas_call(
        functools.partial(densify_kernel, chunks, row_blocks, col_blocks),
        in_specs=[SCALARS] * 3 + [pl.BlockSpec(memory_space=pltpu.HBM)],
        out_specs=WHOLE,
        out_shape=jax.ShapeDtypeStruct((row_blocks * block, col_blocks * block), BF16),
        scratch_shapes=[
            pltpu.VMEM(values.shape, BF16),
            pltpu.VMEM((row_blocks * col_blocks, block, block), F32),
            pltpu.SemaphoreType.DMA((chunks,)),
        ],
        compiler_params=LIMIT,
        cost_estimate=pl.CostEstimate(flops=slots * block * block, bytes_accessed=values.size * 2, transcendentals=0),
        name="densify",
    )(rows, cols, count, values)


def forward_kernel(tile_ref, x0, x1, x2, x3, send_ref, keep_ref):
    row = lax.axis_index("row")
    core = lax.rem(lax.axis_index("col"), 2)
    rows = x0.shape[0]

    def part(block):
        total = None
        for k, x in enumerate((x0, x1, x2, x3)):
            col_at = pl.multiple_of(jnp.bitwise_xor(row, k) * rows, rows)
            tile = tile_ref[pl.ds(pl.multiple_of(block * rows, rows), rows), pl.ds(col_at, rows)]
            term = jnp.dot(tile, x[...], preferred_element_type=F32)
            total = term if total is None else total + term
        return total

    for x in range(2):
        send_ref[pl.ds(x * rows, rows), :] = part(2 * x + 1 - core).astype(BF16)
    for x in range(2):
        keep_ref[pl.ds(x * rows, rows), :] = part(2 * x + core)


def layer_kernel(near_ref, far_ref, cot_ref, cot_far_ref, weight_ref, bias_ref, hidden_ref, swap_ref):
    mine = lax.rem(lax.axis_index("col") // 2, 2)
    rows, hid = cot_ref.shape
    width_in = near_ref.shape[1]
    weight = weight_ref[...]
    gw = None
    gb = None
    for x in range(2):
        block = pl.ds(x * rows, rows)
        aggregate = (near_ref[block, :].astype(F32) + far_ref[block, :].astype(F32)).astype(BF16)
        pre_act = jnp.dot(aggregate, weight, preferred_element_type=F32) + bias_ref[...]
        sigmoid_pre = jax.nn.sigmoid(pre_act)

        @pl.when(mine == x)
        def _():
            hidden_ref[...] = (pre_act * sigmoid_pre).astype(BF16)

        cot = jnp.where(mine == x, cot_ref[...], cot_far_ref[...]).astype(F32)
        pre_grad = (cot * sigmoid_pre * (1.0 + pre_act * (1.0 - sigmoid_pre))).astype(BF16)
        swap_ref[block, :] = lax.dot_general(
            pre_grad, weight, (((1,), (1,)), ((), ())), preferred_element_type=F32
        ).astype(BF16)
        term = lax.dot_general(
            aggregate, pre_grad, (((0,), (0,)), ((), ())), preferred_element_type=F32
        )
        bias_term = jnp.sum(pre_grad.astype(F32), axis=0, keepdims=True)
        gw = term if gw is None else gw + term
        gb = bias_term if gb is None else gb + bias_term
    at = 2 * rows
    for j in range(hid // width_in):
        lanes = slice(j * width_in, (j + 1) * width_in)
        swap_ref[pl.ds(at + j * width_in, width_in), :] = gw[:, lanes].astype(BF16)
    at = at + hid
    swap_ref[pl.ds(at, BIAS_ROWS), :] = jnp.concatenate(
        [gb[:, j * width_in : (j + 1) * width_in] for j in range(hid // width_in)]
        + [jnp.zeros((BIAS_ROWS - hid // width_in, width_in), F32)],
        axis=0,
    ).astype(BF16)


def backward_kernel(tile_ref, own_ref, sib_ref, keep_ref, send1, send2, send3):
    row = lax.axis_index("row")
    core = lax.rem(lax.axis_index("col"), 2)
    rows = keep_ref.shape[0]
    for k, out in ((1, send1), (2, send2), (3, send3), (0, keep_ref)):
        col_at = pl.multiple_of(jnp.bitwise_xor(row, k) * rows, rows)
        total = None
        for half, ref in ((core, own_ref), (1 - core, sib_ref)):
            for x in range(2):
                row_at = pl.multiple_of((2 * x + half) * rows, rows)
                tile = tile_ref[pl.ds(row_at, rows), pl.ds(col_at, rows)]
                term = lax.dot_general(
                    tile, ref[pl.ds(x * rows, rows), :], (((0,), (0,)), ((), ())),
                    preferred_element_type=F32,
                )
                total = term if total is None else total + term
        out[pl.ds(0, rows), :] = total.astype(out.dtype)
    extra = pl.ds(2 * rows, own_ref.shape[0] - 2 * rows)
    send1[pl.ds(rows, send1.shape[0] - rows), :] = (
        own_ref[extra, :].astype(F32) + sib_ref[extra, :].astype(F32)
    ).astype(BF16)


def finish_kernel(scale, near_ref, far_ref, gw_ref, gb_ref):
    width_in, hid = gw_ref.shape
    for j in range(hid // width_in):
        lanes = slice(j * width_in, (j + 1) * width_in)
        block = pl.ds(j * width_in, width_in)
        gw_ref[:, lanes] = (near_ref[block, :].astype(F32) + far_ref[block, :].astype(F32)) * scale
    block = pl.ds(hid, BIAS_ROWS)
    both = (near_ref[block, :].astype(F32) + far_ref[block, :].astype(F32)) * scale
    for j in range(hid // width_in):
        gb_ref[:, j * width_in : (j + 1) * width_in] = both[j : j + 1, :]


def swap(array, axis, bit):
    size = lax.axis_size(axis)
    return lax.ppermute(array, axis, [(i, i ^ bit) for i in range(size)])


def dense_tile(features, block_values, block_rows, block_cols, block_count, weight, bias, cotangent):
    block_size = block_values.shape[1]
    node_rows = cotangent.shape[0]
    width_in = features.shape[1]
    hid = cotangent.shape[1]
    row_blocks = COLS * node_rows // block_size
    col_blocks = ROWS * node_rows // block_size
    extra = hid + BIAS_ROWS
    shards = [features] + [swap(features, "row", k) for k in (1, 2, 3)]
    shards, cot_far = lax.optimization_barrier((shards, swap(cotangent, "col", 2)))
    tile = densify(block_values, block_rows, block_cols, block_count, row_blocks, col_blocks)
    half = (2 * node_rows, width_in)
    send, keep = pl.pallas_call(
        forward_kernel,
        in_specs=[WHOLE] * 5,
        out_specs=[WHOLE] * 2,
        out_shape=[jax.ShapeDtypeStruct(half, BF16), jax.ShapeDtypeStruct(half, F32)],
        compiler_params=LIMIT,
        name="forward",
    )(tile, *shards)
    near = (keep + swap(send, "col", 1).astype(F32)).astype(BF16)
    far = swap(near, "col", 2)
    hidden, grads = pl.pallas_call(
        layer_kernel,
        in_specs=[WHOLE] * 6,
        out_specs=[WHOLE] * 2,
        out_shape=[
            jax.ShapeDtypeStruct((node_rows, hid), BF16),
            jax.ShapeDtypeStruct((2 * node_rows + extra, width_in), BF16),
        ],
        compiler_params=LIMIT,
        name="layer",
    )(near, far, cotangent, cot_far, weight, bias.reshape(1, hid))
    block = jax.ShapeDtypeStruct((node_rows, width_in), BF16)
    own, *sends = pl.pallas_call(
        backward_kernel,
        in_specs=[WHOLE] * 3,
        out_specs=[WHOLE] * 4,
        out_shape=[
            jax.ShapeDtypeStruct(block.shape, F32),
            jax.ShapeDtypeStruct((node_rows + extra, width_in), BF16),
            block,
            block,
        ],
        compiler_params=LIMIT,
        name="backward",
    )(tile, grads, swap(grads, "col", 1))
    got = [swap(part, "row", k) for k, part in zip((1, 2, 3), sends)]
    pair = (sends[0][node_rows:].astype(F32) + got[0][node_rows:].astype(F32)).astype(BF16)
    pair_far = swap(pair, "row", 2)
    grad_features = (
        own + got[0][:node_rows].astype(F32) + got[1].astype(F32) + got[2].astype(F32)
    ).astype(BF16)
    norm_scale = float(node_rows * ROWS * COLS) ** (-0.5)
    grad_weight, grad_bias = pl.pallas_call(
        functools.partial(finish_kernel, norm_scale),
        in_specs=[WHOLE] * 2,
        out_specs=[WHOLE] * 2,
        out_shape=[
            jax.ShapeDtypeStruct((width_in, hid), F32),
            jax.ShapeDtypeStruct((1, hid), F32),
        ],
        compiler_params=LIMIT,
        name="finish",
    )(pair, pair_far)
    return hidden, grad_weight, grad_bias.reshape(hid), grad_features


def solution(mesh):
    in_specs = (
        P(("parts", "col", "row"), None),
        P(("parts", "row", "col"), None, None),
        P(("parts", "row", "col")),
        P(("parts", "row", "col")),
        P(("parts", "row", "col")),
        P(),
        P(),
        P(("parts", "row", "col"), None),
    )
    out_specs = (
        P(("parts", "row", "col"), None),
        P("parts", None),
        P("parts"),
        P(("parts", "col", "row"), None),
    )
    small = mesh.shape["row"] == ROWS and mesh.shape["col"] == COLS
    return jax.shard_map(
        dense_tile if small else by_slots,
        mesh=mesh,
        in_specs=in_specs,
        out_specs=out_specs,
        check_vma=False,
    )
```

```python
import functools

import jax
import jax.numpy as jnp
from jax import lax
from jax.experimental import pallas as pl
from jax.experimental.pallas import tpu as pltpu
from jax.sharding import PartitionSpec as P

F32 = jnp.float32
BF16 = jnp.bfloat16
ROWS = 4
COLS = 4
WHOLE = pl.BlockSpec(memory_space=pltpu.VMEM)
SCALARS = pl.BlockSpec(memory_space=pltpu.SMEM)
LIMIT = pltpu.CompilerParams(vmem_limit_bytes=16 * 2**20)
BIAS_ROWS = 16
GROUP = 4


def pick_rows(pick_index, live_mask, source_rows):
    source_count = source_rows.shape[0]
    onehot = (
        (pick_index[:, None] == jnp.arange(source_count, dtype=jnp.int32)[None, :])
        & live_mask[:, None]
    ).astype(jnp.bfloat16)
    chosen = jnp.dot(
        onehot, source_rows.reshape(source_count, -1), preferred_element_type=jnp.float32
    ).astype(jnp.bfloat16)
    return chosen.reshape((pick_index.shape[0],) + source_rows.shape[1:])


def slot_terms(values, pick_index, live_mask, source_rows, forward_pass):
    chosen = pick_rows(pick_index, live_mask, source_rows)
    if forward_pass:
        return jnp.einsum("spq,sqf->spf", values, chosen, preferred_element_type=jnp.float32)
    return jnp.einsum("spq,spf->sqf", values, chosen, preferred_element_type=jnp.float32)


def place_terms(products, place_index, blocks):
    block_ids = jnp.arange(blocks, dtype=jnp.int32)
    onehot = (block_ids[:, None] == place_index[None, :]).astype(jnp.bfloat16)
    flat = products.reshape(products.shape[0], -1)
    upper = flat.astype(jnp.bfloat16)
    lower = (flat - upper.astype(jnp.float32)).astype(jnp.bfloat16)
    placed = jnp.dot(onehot, upper, preferred_element_type=jnp.float32)
    placed = placed + jnp.dot(onehot, lower, preferred_element_type=jnp.float32)
    return placed.reshape(blocks * products.shape[1], products.shape[2])


def by_slots(features, block_values, block_rows, block_cols, block_count, weight, bias, cotangent):
    block_size = block_values.shape[1]
    slot_total = block_values.shape[0]
    live_mask = jnp.arange(slot_total, dtype=jnp.int32) < block_count[0]
    node_rows = cotangent.shape[0]
    width_in = features.shape[1]
    column_rows = lax.all_gather(features, "row", axis=0, tiled=True)
    column_blocks = column_rows.reshape(-1, block_size, width_in)
    forward_terms = slot_terms(block_values, block_cols, live_mask, column_blocks, True)
    aggregate = lax.psum_scatter(
        place_terms(
            forward_terms, block_rows, lax.axis_size("col") * node_rows // block_size
        ).astype(jnp.bfloat16),
        "col",
        scatter_dimension=0,
        tiled=True,
    ).astype(jnp.float32)
    aggregate = aggregate.astype(jnp.bfloat16)
    pre_act = jnp.dot(aggregate, weight, preferred_element_type=jnp.float32) + bias
    sigmoid_pre = jax.nn.sigmoid(pre_act)
    hidden = (pre_act * sigmoid_pre).astype(jnp.bfloat16)
    pre_grad = (
        cotangent.astype(jnp.float32) * sigmoid_pre * (1.0 + pre_act * (1.0 - sigmoid_pre))
    ).astype(jnp.bfloat16)
    grad_local = lax.dot_general(
        aggregate, pre_grad, (((0,), (0,)), ((), ())), preferred_element_type=jnp.float32
    )
    bias_local = jnp.sum(pre_grad.astype(jnp.float32), axis=0)
    grad_weight, grad_bias = lax.psum((grad_local, bias_local), ("row", "col"))
    norm_scale = float(node_rows * lax.axis_size("row") * lax.axis_size("col")) ** (-0.5)
    agg_grad = lax.dot_general(
        pre_grad, weight, (((1,), (1,)), ((), ())), preferred_element_type=jnp.float32
    ).astype(jnp.bfloat16)
    stripe_rows = lax.all_gather(agg_grad, "col", axis=0, tiled=True)
    stripe_blocks = stripe_rows.reshape(-1, block_size, width_in)
    backward_terms = slot_terms(block_values, block_rows, live_mask, stripe_blocks, False)
    grad_features = lax.psum_scatter(
        place_terms(
            backward_terms, block_cols, lax.axis_size("row") * node_rows // block_size
        ).astype(jnp.bfloat16),
        "row",
        scatter_dimension=0,
        tiled=True,
    )
    return (hidden, grad_weight * norm_scale, grad_bias * norm_scale, grad_features)


def densify_kernel(chunks, row_blocks, col_blocks, count_in, rows_in, cols_in, values_ref, tile_ref,
                   held, acc, count_ref, rows_ref, cols_ref, sems, scalar_sems):
    slots, block, _ = values_ref.shape
    size = slots // chunks
    scalars = [
        pltpu.make_async_copy(source, held_in, scalar_sems.at[i])
        for i, (source, held_in) in enumerate(
            ((count_in, count_ref), (rows_in, rows_ref), (cols_in, cols_ref))
        )
    ]
    copies = [
        pltpu.make_async_copy(
            values_ref.at[pl.ds(i * size, size)], held.at[pl.ds(i * size, size)], sems.at[i]
        )
        for i in range(chunks)
    ]
    for copy in scalars + copies:
        copy.start()
    acc[...] = jnp.zeros_like(acc)
    for copy in scalars:
        copy.wait()
    live = count_ref[0, 0]

    def add_slot(i, carry):
        place = rows_ref[i] * col_blocks + cols_ref[i]
        acc[place] = acc[place] + held[i].astype(F32)
        return carry

    def add_group(first, i, carry):
        for j in range(GROUP):
            add_slot(first + i * GROUP + j, carry)
        return carry

    for i, copy in enumerate(copies):
        copy.wait()
        here = jnp.clip(live - i * size, 0, size)
        groups = here // GROUP
        lax.fori_loop(0, groups, functools.partial(add_group, i * size), 0)
        lax.fori_loop(i * size + groups * GROUP, i * size + here, add_slot, 0)
    for r in range(row_blocks):
        for c in range(col_blocks):
            tile_ref[pl.ds(r * block, block), pl.ds(c * block, block)] = acc[
                r * col_blocks + c
            ].astype(BF16)


def densify(values, rows, cols, count, row_blocks, col_blocks):
    slots, block, _ = values.shape
    chunks = 8
    in_hbm = [
        pltpu.with_memory_space_constraint(array, pltpu.HBM)
        for array in (rows, cols, values)
    ]
    return pl.pallas_call(
        functools.partial(densify_kernel, chunks, row_blocks, col_blocks),
        in_specs=[WHOLE] + [pl.BlockSpec(memory_space=pltpu.HBM)] * 3,
        out_specs=WHOLE,
        out_shape=jax.ShapeDtypeStruct((row_blocks * block, col_blocks * block), BF16),
        scratch_shapes=[
            pltpu.VMEM(values.shape, BF16),
            pltpu.VMEM((row_blocks * col_blocks, block, block), F32),
            pltpu.SMEM((1, 1), jnp.int32),
            pltpu.SMEM(rows.shape, jnp.int32),
            pltpu.SMEM(cols.shape, jnp.int32),
            pltpu.SemaphoreType.DMA((chunks,)),
            pltpu.SemaphoreType.DMA((3,)),
        ],
        compiler_params=LIMIT,
        cost_estimate=pl.CostEstimate(flops=slots * block * block, bytes_accessed=values.size * 2, transcendentals=0),
        name="densify",
    )(count.reshape(1, 1), *in_hbm)


def forward_kernel(tile_ref, x0, x1, x2, x3, send_ref, keep_ref):
    row = lax.axis_index("row")
    core = lax.rem(lax.axis_index("col"), 2)
    rows = x0.shape[0]

    def part(block):
        total = None
        for k, x in enumerate((x0, x1, x2, x3)):
            col_at = pl.multiple_of(jnp.bitwise_xor(row, k) * rows, rows)
            tile = tile_ref[pl.ds(pl.multiple_of(block * rows, rows), rows), pl.ds(col_at, rows)]
            term = jnp.dot(tile, x[...], preferred_element_type=F32)
            total = term if total is None else total + term
        return total

    for x in range(2):
        send_ref[pl.ds(x * rows, rows), :] = part(2 * x + 1 - core).astype(BF16)
    for x in range(2):
        keep_ref[pl.ds(x * rows, rows), :] = part(2 * x + core)


def layer_kernel(near_ref, far_ref, cot_ref, cot_far_ref, weight_ref, bias_ref, hidden_ref, swap_ref):
    mine = lax.rem(lax.axis_index("col") // 2, 2)
    rows, hid = cot_ref.shape
    width_in = near_ref.shape[1]
    weight = weight_ref[...]
    gw = None
    gb = None
    for x in range(2):
        block = pl.ds(x * rows, rows)
        aggregate = (near_ref[block, :].astype(F32) + far_ref[block, :].astype(F32)).astype(BF16)
        pre_act = jnp.dot(aggregate, weight, preferred_element_type=F32) + bias_ref[...]
        sigmoid_pre = jax.nn.sigmoid(pre_act)

        @pl.when(mine == x)
        def _():
            hidden_ref[...] = (pre_act * sigmoid_pre).astype(BF16)

        cot = jnp.where(mine == x, cot_ref[...], cot_far_ref[...]).astype(F32)
        pre_grad = (cot * sigmoid_pre * (1.0 + pre_act * (1.0 - sigmoid_pre))).astype(BF16)
        swap_ref[block, :] = lax.dot_general(
            pre_grad, weight, (((1,), (1,)), ((), ())), preferred_element_type=F32
        ).astype(BF16)
        term = lax.dot_general(
            aggregate, pre_grad, (((0,), (0,)), ((), ())), preferred_element_type=F32
        )
        bias_term = jnp.sum(pre_grad.astype(F32), axis=0, keepdims=True)
        gw = term if gw is None else gw + term
        gb = bias_term if gb is None else gb + bias_term
    at = 2 * rows
    for j in range(hid // width_in):
        lanes = slice(j * width_in, (j + 1) * width_in)
        swap_ref[pl.ds(at + j * width_in, width_in), :] = gw[:, lanes].astype(BF16)
    at = at + hid
    swap_ref[pl.ds(at, BIAS_ROWS), :] = jnp.concatenate(
        [gb[:, j * width_in : (j + 1) * width_in] for j in range(hid // width_in)]
        + [jnp.zeros((BIAS_ROWS - hid // width_in, width_in), F32)],
        axis=0,
    ).astype(BF16)


def backward_terms(tile_ref, half, k, grad_ref, rows):
    col_at = pl.multiple_of(jnp.bitwise_xor(lax.axis_index("row"), k) * rows, rows)
    total = None
    for x in range(2):
        row_at = pl.multiple_of((2 * x + half) * rows, rows)
        term = lax.dot_general(
            tile_ref[pl.ds(row_at, rows), pl.ds(col_at, rows)],
            grad_ref[pl.ds(x * rows, rows), :],
            (((0,), (0,)), ((), ())),
            preferred_element_type=F32,
        )
        total = term if total is None else total + term
    return total


def backward_mine_kernel(tile_ref, own_ref, part_ref):
    core = lax.rem(lax.axis_index("col"), 2)
    for k in range(ROWS):
        part_ref[k] = backward_terms(tile_ref, core, k, own_ref, part_ref.shape[1])


def backward_kernel(tile_ref, own_ref, sib_ref, part_ref, keep_ref, send1, send2, send3):
    core = lax.rem(lax.axis_index("col"), 2)
    rows = keep_ref.shape[0]
    for k, out in ((1, send1), (2, send2), (3, send3), (0, keep_ref)):
        total = part_ref[k] + backward_terms(tile_ref, 1 - core, k, sib_ref, rows)
        out[pl.ds(0, rows), :] = total.astype(out.dtype)
    extra = pl.ds(2 * rows, own_ref.shape[0] - 2 * rows)
    send1[pl.ds(rows, send1.shape[0] - rows), :] = (
        own_ref[extra, :].astype(F32) + sib_ref[extra, :].astype(F32)
    ).astype(BF16)


def finish_kernel(scale, near_ref, far_ref, gw_ref, gb_ref):
    width_in, hid = gw_ref.shape
    for j in range(hid // width_in):
        lanes = slice(j * width_in, (j + 1) * width_in)
        block = pl.ds(j * width_in, width_in)
        gw_ref[:, lanes] = (near_ref[block, :].astype(F32) + far_ref[block, :].astype(F32)) * scale
    block = pl.ds(hid, BIAS_ROWS)
    both = (near_ref[block, :].astype(F32) + far_ref[block, :].astype(F32)) * scale
    for j in range(hid // width_in):
        gb_ref[:, j * width_in : (j + 1) * width_in] = both[j : j + 1, :]


def swap(array, axis, bit):
    size = lax.axis_size(axis)
    return lax.ppermute(array, axis, [(i, i ^ bit) for i in range(size)])


def dense_tile(features, block_values, block_rows, block_cols, block_count, weight, bias, cotangent):
    block_size = block_values.shape[1]
    node_rows = cotangent.shape[0]
    width_in = features.shape[1]
    hid = cotangent.shape[1]
    row_blocks = COLS * node_rows // block_size
    col_blocks = ROWS * node_rows // block_size
    extra = hid + BIAS_ROWS
    shards = [features] + [swap(features, "row", k) for k in (1, 2, 3)]
    tile = densify(block_values, block_rows, block_cols, block_count, row_blocks, col_blocks)
    tile, shards[1], cotangent = lax.optimization_barrier((tile, shards[1], cotangent))
    cot_far = swap(cotangent, "col", 2)
    half = (2 * node_rows, width_in)
    send, keep = pl.pallas_call(
        forward_kernel,
        in_specs=[WHOLE] * 5,
        out_specs=[WHOLE] * 2,
        out_shape=[jax.ShapeDtypeStruct(half, BF16), jax.ShapeDtypeStruct(half, F32)],
        compiler_params=LIMIT,
        name="forward",
    )(tile, *shards)
    sib, cot_far = lax.optimization_barrier((swap(send, "col", 1), cot_far))
    near = (keep + sib.astype(F32)).astype(BF16)
    far = swap(near, "col", 2)
    hidden, grads = pl.pallas_call(
        layer_kernel,
        in_specs=[WHOLE] * 6,
        out_specs=[WHOLE] * 2,
        out_shape=[
            jax.ShapeDtypeStruct((node_rows, hid), BF16),
            jax.ShapeDtypeStruct((2 * node_rows + extra, width_in), BF16),
        ],
        compiler_params=LIMIT,
        name="layer",
    )(near, far, cotangent, cot_far, weight, bias.reshape(1, hid))
    block = jax.ShapeDtypeStruct((node_rows, width_in), BF16)
    part = pl.pallas_call(
        backward_mine_kernel,
        in_specs=[WHOLE] * 2,
        out_specs=WHOLE,
        out_shape=jax.ShapeDtypeStruct((ROWS, node_rows, width_in), F32),
        compiler_params=LIMIT,
        cost_estimate=pl.CostEstimate(flops=tile.size * width_in, bytes_accessed=tile.size, transcendentals=0),
        name="backward_mine",
    )(tile, grads)
    own, *sends = pl.pallas_call(
        backward_kernel,
        in_specs=[WHOLE] * 4,
        out_specs=[WHOLE] * 4,
        out_shape=[
            jax.ShapeDtypeStruct(block.shape, F32),
            jax.ShapeDtypeStruct((node_rows + extra, width_in), BF16),
            block,
            block,
        ],
        compiler_params=LIMIT,
        name="backward",
    )(tile, grads, swap(grads, "col", 1), part)
    got = [swap(part, "row", k) for k, part in zip((1, 2, 3), sends)]
    pair = (sends[0][node_rows:].astype(F32) + got[0][node_rows:].astype(F32)).astype(BF16)
    pair_far = swap(pair, "row", 2)
    grad_features = (
        own + got[0][:node_rows].astype(F32) + got[1].astype(F32) + got[2].astype(F32)
    ).astype(BF16)
    norm_scale = float(node_rows * ROWS * COLS) ** (-0.5)
    grad_weight, grad_bias = pl.pallas_call(
        functools.partial(finish_kernel, norm_scale),
        in_specs=[WHOLE] * 2,
        out_specs=[WHOLE] * 2,
        out_shape=[
            jax.ShapeDtypeStruct((width_in, hid), F32),
            jax.ShapeDtypeStruct((1, hid), F32),
        ],
        compiler_params=LIMIT,
        name="finish",
    )(pair, pair_far)
    return hidden, grad_weight, grad_bias.reshape(hid), grad_features


def solution(mesh):
    in_specs = (
        P(("parts", "col", "row"), None),
        P(("parts", "row", "col"), None, None),
        P(("parts", "row", "col")),
        P(("parts", "row", "col")),
        P(("parts", "row", "col")),
        P(),
        P(),
        P(("parts", "row", "col"), None),
    )
    out_specs = (
        P(("parts", "row", "col"), None),
        P("parts", None),
        P("parts"),
        P(("parts", "col", "row"), None),
    )
    small = mesh.shape["row"] == ROWS and mesh.shape["col"] == COLS
    return jax.shard_map(
        dense_tile if small else by_slots,
        mesh=mesh,
        in_specs=in_specs,
        out_specs=out_specs,
        check_vma=False,
    )
```

```python
import functools

import jax
import jax.numpy as jnp
from jax import lax
from jax.experimental import pallas as pl
from jax.experimental.pallas import tpu as pltpu
from jax.sharding import PartitionSpec as P

F32 = jnp.float32
BF16 = jnp.bfloat16
ROWS = 4
COLS = 4
WHOLE = pl.BlockSpec(memory_space=pltpu.VMEM)
SCALARS = pl.BlockSpec(memory_space=pltpu.SMEM)
LIMIT = pltpu.CompilerParams(vmem_limit_bytes=16 * 2**20)
BIAS_ROWS = 16
GROUP = 4


def pick_rows(pick_index, live_mask, source_rows):
    source_count = source_rows.shape[0]
    onehot = (
        (pick_index[:, None] == jnp.arange(source_count, dtype=jnp.int32)[None, :])
        & live_mask[:, None]
    ).astype(jnp.bfloat16)
    chosen = jnp.dot(
        onehot, source_rows.reshape(source_count, -1), preferred_element_type=jnp.float32
    ).astype(jnp.bfloat16)
    return chosen.reshape((pick_index.shape[0],) + source_rows.shape[1:])


def slot_terms(values, pick_index, live_mask, source_rows, forward_pass):
    chosen = pick_rows(pick_index, live_mask, source_rows)
    if forward_pass:
        return jnp.einsum("spq,sqf->spf", values, chosen, preferred_element_type=jnp.float32)
    return jnp.einsum("spq,spf->sqf", values, chosen, preferred_element_type=jnp.float32)


def place_terms(products, place_index, blocks):
    block_ids = jnp.arange(blocks, dtype=jnp.int32)
    onehot = (block_ids[:, None] == place_index[None, :]).astype(jnp.bfloat16)
    flat = products.reshape(products.shape[0], -1)
    upper = flat.astype(jnp.bfloat16)
    lower = (flat - upper.astype(jnp.float32)).astype(jnp.bfloat16)
    placed = jnp.dot(onehot, upper, preferred_element_type=jnp.float32)
    placed = placed + jnp.dot(onehot, lower, preferred_element_type=jnp.float32)
    return placed.reshape(blocks * products.shape[1], products.shape[2])


def by_slots(features, block_values, block_rows, block_cols, block_count, weight, bias, cotangent):
    block_size = block_values.shape[1]
    slot_total = block_values.shape[0]
    live_mask = jnp.arange(slot_total, dtype=jnp.int32) < block_count[0]
    node_rows = cotangent.shape[0]
    width_in = features.shape[1]
    column_rows = lax.all_gather(features, "row", axis=0, tiled=True)
    column_blocks = column_rows.reshape(-1, block_size, width_in)
    forward_terms = slot_terms(block_values, block_cols, live_mask, column_blocks, True)
    aggregate = lax.psum_scatter(
        place_terms(
            forward_terms, block_rows, lax.axis_size("col") * node_rows // block_size
        ).astype(jnp.bfloat16),
        "col",
        scatter_dimension=0,
        tiled=True,
    ).astype(jnp.float32)
    aggregate = aggregate.astype(jnp.bfloat16)
    pre_act = jnp.dot(aggregate, weight, preferred_element_type=jnp.float32) + bias
    sigmoid_pre = jax.nn.sigmoid(pre_act)
    hidden = (pre_act * sigmoid_pre).astype(jnp.bfloat16)
    pre_grad = (
        cotangent.astype(jnp.float32) * sigmoid_pre * (1.0 + pre_act * (1.0 - sigmoid_pre))
    ).astype(jnp.bfloat16)
    grad_local = lax.dot_general(
        aggregate, pre_grad, (((0,), (0,)), ((), ())), preferred_element_type=jnp.float32
    )
    bias_local = jnp.sum(pre_grad.astype(jnp.float32), axis=0)
    grad_weight, grad_bias = lax.psum((grad_local, bias_local), ("row", "col"))
    norm_scale = float(node_rows * lax.axis_size("row") * lax.axis_size("col")) ** (-0.5)
    agg_grad = lax.dot_general(
        pre_grad, weight, (((1,), (1,)), ((), ())), preferred_element_type=jnp.float32
    ).astype(jnp.bfloat16)
    stripe_rows = lax.all_gather(agg_grad, "col", axis=0, tiled=True)
    stripe_blocks = stripe_rows.reshape(-1, block_size, width_in)
    backward_terms = slot_terms(block_values, block_rows, live_mask, stripe_blocks, False)
    grad_features = lax.psum_scatter(
        place_terms(
            backward_terms, block_cols, lax.axis_size("row") * node_rows // block_size
        ).astype(jnp.bfloat16),
        "row",
        scatter_dimension=0,
        tiled=True,
    )
    return (hidden, grad_weight * norm_scale, grad_bias * norm_scale, grad_features)


def densify_kernel(chunks, row_blocks, col_blocks, count_in, rows_in, cols_in, values_ref, tile_ref,
                   held, acc, count_ref, rows_ref, cols_ref, sems, scalar_sems):
    slots, block, _ = values_ref.shape
    size = slots // chunks
    scalars = [
        pltpu.make_async_copy(source, held_in, scalar_sems.at[i])
        for i, (source, held_in) in enumerate(
            ((count_in, count_ref), (rows_in, rows_ref), (cols_in, cols_ref))
        )
    ]
    copies = [
        pltpu.make_async_copy(
            values_ref.at[pl.ds(i * size, size)], held.at[pl.ds(i * size, size)], sems.at[i]
        )
        for i in range(chunks)
    ]
    for copy in scalars + copies:
        copy.start()
    acc[...] = jnp.zeros_like(acc)
    for copy in scalars:
        copy.wait()
    live = count_ref[0, 0]

    def add_slot(i, carry):
        place = rows_ref[i] * col_blocks + cols_ref[i]
        acc[place] = acc[place] + held[i].astype(F32)
        return carry

    def add_group(first, i, carry):
        for j in range(GROUP):
            add_slot(first + i * GROUP + j, carry)
        return carry

    for i, copy in enumerate(copies):
        copy.wait()
        here = jnp.clip(live - i * size, 0, size)
        groups = here // GROUP
        lax.fori_loop(0, groups, functools.partial(add_group, i * size), 0)
        lax.fori_loop(i * size + groups * GROUP, i * size + here, add_slot, 0)
    for r in range(row_blocks):
        for c in range(col_blocks):
            tile_ref[pl.ds(r * block, block), pl.ds(c * block, block)] = acc[
                r * col_blocks + c
            ].astype(BF16)


def densify(values, rows, cols, count, row_blocks, col_blocks):
    slots, block, _ = values.shape
    chunks = 8
    in_hbm = [
        pltpu.with_memory_space_constraint(array, pltpu.HBM)
        for array in (rows, cols, values)
    ]
    return pl.pallas_call(
        functools.partial(densify_kernel, chunks, row_blocks, col_blocks),
        in_specs=[WHOLE] + [pl.BlockSpec(memory_space=pltpu.HBM)] * 3,
        out_specs=WHOLE,
        out_shape=jax.ShapeDtypeStruct((row_blocks * block, col_blocks * block), BF16),
        scratch_shapes=[
            pltpu.VMEM(values.shape, BF16),
            pltpu.VMEM((row_blocks * col_blocks, block, block), F32),
            pltpu.SMEM((1, 1), jnp.int32),
            pltpu.SMEM(rows.shape, jnp.int32),
            pltpu.SMEM(cols.shape, jnp.int32),
            pltpu.SemaphoreType.DMA((chunks,)),
            pltpu.SemaphoreType.DMA((3,)),
        ],
        compiler_params=LIMIT,
        cost_estimate=pl.CostEstimate(flops=slots * block * block, bytes_accessed=values.size * 2, transcendentals=0),
        name="densify",
    )(count.reshape(1, 1), *in_hbm)


def forward_kernel(tile_ref, outer_ref, x1, x2, send_ref, keep_ref):
    row = lax.axis_index("row")
    core = lax.rem(lax.axis_index("col"), 2)
    rows = x1.shape[0]

    def part(block):
        total = None
        for k, shard in ((0, outer_ref[:rows, :]), (3, outer_ref[rows:, :]), (1, x1[...]), (2, x2[...])):
            col_at = pl.multiple_of(jnp.bitwise_xor(row, k) * rows, rows)
            tile = tile_ref[pl.ds(pl.multiple_of(block * rows, rows), rows), pl.ds(col_at, rows)]
            term = jnp.dot(tile, shard, preferred_element_type=F32)
            total = term if total is None else total + term
        return total

    for x in range(2):
        send_ref[pl.ds(x * rows, rows), :] = part(2 * x + 1 - core).astype(BF16)
    for x in range(2):
        keep_ref[pl.ds(x * rows, rows), :] = part(2 * x + core)


def layer_kernel(near_ref, far_ref, cot_ref, cot_far_ref, weight_ref, bias_ref, hidden_ref, swap_ref):
    mine = lax.rem(lax.axis_index("col") // 2, 2)
    rows, hid = cot_ref.shape
    width_in = near_ref.shape[1]
    weight = weight_ref[...]
    gw = None
    gb = None
    for x in range(2):
        block = pl.ds(x * rows, rows)
        aggregate = (near_ref[block, :].astype(F32) + far_ref[block, :].astype(F32)).astype(BF16)
        pre_act = jnp.dot(aggregate, weight, preferred_element_type=F32) + bias_ref[...]
        sigmoid_pre = jax.nn.sigmoid(pre_act)

        @pl.when(mine == x)
        def _():
            hidden_ref[...] = (pre_act * sigmoid_pre).astype(BF16)

        cot = jnp.where(mine == x, cot_ref[...], cot_far_ref[...]).astype(F32)
        pre_grad = (cot * sigmoid_pre * (1.0 + pre_act * (1.0 - sigmoid_pre))).astype(BF16)
        swap_ref[block, :] = lax.dot_general(
            pre_grad, weight, (((1,), (1,)), ((), ())), preferred_element_type=F32
        ).astype(BF16)
        term = lax.dot_general(
            aggregate, pre_grad, (((0,), (0,)), ((), ())), preferred_element_type=F32
        )
        bias_term = jnp.sum(pre_grad.astype(F32), axis=0, keepdims=True)
        gw = term if gw is None else gw + term
        gb = bias_term if gb is None else gb + bias_term
    at = 2 * rows
    for j in range(hid // width_in):
        lanes = slice(j * width_in, (j + 1) * width_in)
        swap_ref[pl.ds(at + j * width_in, width_in), :] = gw[:, lanes].astype(BF16)
    at = at + hid
    swap_ref[pl.ds(at, BIAS_ROWS), :] = jnp.concatenate(
        [gb[:, j * width_in : (j + 1) * width_in] for j in range(hid // width_in)]
        + [jnp.zeros((BIAS_ROWS - hid // width_in, width_in), F32)],
        axis=0,
    ).astype(BF16)


def backward_terms(tile_ref, half, k, grad_ref, rows):
    col_at = pl.multiple_of(jnp.bitwise_xor(lax.axis_index("row"), k) * rows, rows)
    total = None
    for x in range(2):
        row_at = pl.multiple_of((2 * x + half) * rows, rows)
        term = lax.dot_general(
            tile_ref[pl.ds(row_at, rows), pl.ds(col_at, rows)],
            grad_ref[pl.ds(x * rows, rows), :],
            (((0,), (0,)), ((), ())),
            preferred_element_type=F32,
        )
        total = term if total is None else total + term
    return total


def backward_mine_kernel(tile_ref, own_ref, part_ref):
    core = lax.rem(lax.axis_index("col"), 2)
    for k in range(ROWS):
        part_ref[k] = backward_terms(tile_ref, core, k, own_ref, part_ref.shape[1])


def backward_kernel(tile_ref, own_ref, sib_ref, part_ref, keep_ref, send1, send2, send3):
    core = lax.rem(lax.axis_index("col"), 2)
    rows = keep_ref.shape[0]
    for k, out in ((1, send1), (2, send2), (3, send3), (0, keep_ref)):
        total = part_ref[k] + backward_terms(tile_ref, 1 - core, k, sib_ref, rows)
        out[pl.ds(0, rows), :] = total.astype(out.dtype)
    extra = pl.ds(2 * rows, own_ref.shape[0] - 2 * rows)
    send1[pl.ds(rows, send1.shape[0] - rows), :] = (
        own_ref[extra, :].astype(F32) + sib_ref[extra, :].astype(F32)
    ).astype(BF16)


def write_kernel(source_ref, out_ref):
    out_ref[...] = source_ref[...]


def finish_kernel(scale, near_ref, far_ref, gw_ref, gb_ref):
    width_in, hid = gw_ref.shape
    for j in range(hid // width_in):
        lanes = slice(j * width_in, (j + 1) * width_in)
        block = pl.ds(j * width_in, width_in)
        gw_ref[:, lanes] = (near_ref[block, :].astype(F32) + far_ref[block, :].astype(F32)) * scale
    block = pl.ds(hid, BIAS_ROWS)
    both = (near_ref[block, :].astype(F32) + far_ref[block, :].astype(F32)) * scale
    for j in range(hid // width_in):
        gb_ref[:, j * width_in : (j + 1) * width_in] = both[j : j + 1, :]


def swap(array, axis, bit):
    size = lax.axis_size(axis)
    return lax.ppermute(array, axis, [(i, i ^ bit) for i in range(size)])


def dense_tile(features, block_values, block_rows, block_cols, block_count, weight, bias, cotangent):
    block_size = block_values.shape[1]
    node_rows = cotangent.shape[0]
    width_in = features.shape[1]
    hid = cotangent.shape[1]
    row_blocks = COLS * node_rows // block_size
    col_blocks = ROWS * node_rows // block_size
    extra = hid + BIAS_ROWS
    shards = [swap(features, "row", k) for k in (1, 2)]
    outer = jnp.concatenate([features, swap(features, "row", 3)])
    tile = densify(block_values, block_rows, block_cols, block_count, row_blocks, col_blocks)
    cot_far = swap(cotangent, "col", 2)
    half = (2 * node_rows, width_in)
    send, keep = pl.pallas_call(
        forward_kernel,
        in_specs=[WHOLE] * 4,
        out_specs=[WHOLE] * 2,
        out_shape=[jax.ShapeDtypeStruct(half, BF16), jax.ShapeDtypeStruct(half, F32)],
        compiler_params=LIMIT,
        name="forward",
    )(tile, outer, *shards)
    sib, cot_far = lax.optimization_barrier((swap(send, "col", 1), cot_far))
    near = (keep + sib.astype(F32)).astype(BF16)
    far = swap(near, "col", 2)
    hidden, grads = pl.pallas_call(
        layer_kernel,
        in_specs=[WHOLE] * 6,
        out_specs=[WHOLE] * 2,
        out_shape=[
            pltpu.VMEM((node_rows, hid), BF16),
            jax.ShapeDtypeStruct((2 * node_rows + extra, width_in), BF16),
        ],
        compiler_params=LIMIT,
        name="layer",
    )(near, far, cotangent, cot_far, weight, bias.reshape(1, hid))
    block = jax.ShapeDtypeStruct((node_rows, width_in), BF16)
    part = pl.pallas_call(
        backward_mine_kernel,
        in_specs=[WHOLE] * 2,
        out_specs=WHOLE,
        out_shape=jax.ShapeDtypeStruct((ROWS, node_rows, width_in), F32),
        compiler_params=LIMIT,
        cost_estimate=pl.CostEstimate(flops=tile.size * width_in, bytes_accessed=tile.size, transcendentals=0),
        name="backward_mine",
    )(tile, grads)
    own, *sends = pl.pallas_call(
        backward_kernel,
        in_specs=[WHOLE] * 4,
        out_specs=[WHOLE] * 4,
        out_shape=[
            jax.ShapeDtypeStruct(block.shape, F32),
            jax.ShapeDtypeStruct((node_rows + extra, width_in), BF16),
            block,
            block,
        ],
        compiler_params=LIMIT,
        name="backward",
    )(tile, grads, swap(grads, "col", 1), part)
    got = [swap(part, "row", k) for k, part in zip((1, 2, 3), sends)]
    pair = (sends[0][node_rows:].astype(F32) + got[0][node_rows:].astype(F32)).astype(BF16)
    pair_far = swap(pair, "row", 2)
    grad_features = (
        own + got[0][:node_rows].astype(F32) + got[1].astype(F32) + got[2].astype(F32)
    ).astype(BF16)
    grad_features, hidden = lax.optimization_barrier((grad_features, hidden))
    hidden = pl.pallas_call(
        write_kernel,
        in_specs=[WHOLE],
        out_specs=WHOLE,
        out_shape=jax.ShapeDtypeStruct(hidden.shape, BF16),
        compiler_params=LIMIT,
        name="write_hidden",
    )(hidden)
    norm_scale = float(node_rows * ROWS * COLS) ** (-0.5)
    grad_weight, grad_bias = pl.pallas_call(
        functools.partial(finish_kernel, norm_scale),
        in_specs=[WHOLE] * 2,
        out_specs=[WHOLE] * 2,
        out_shape=[
            jax.ShapeDtypeStruct((width_in, hid), F32),
            jax.ShapeDtypeStruct((1, hid), F32),
        ],
        compiler_params=LIMIT,
        name="finish",
    )(pair, pair_far)
    return hidden, grad_weight, grad_bias.reshape(hid), grad_features


def solution(mesh):
    in_specs = (
        P(("parts", "col", "row"), None),
        P(("parts", "row", "col"), None, None),
        P(("parts", "row", "col")),
        P(("parts", "row", "col")),
        P(("parts", "row", "col")),
        P(),
        P(),
        P(("parts", "row", "col"), None),
    )
    out_specs = (
        P(("parts", "row", "col"), None),
        P("parts", None),
        P("parts"),
        P(("parts", "col", "row"), None),
    )
    small = mesh.shape["row"] == ROWS and mesh.shape["col"] == COLS
    return jax.shard_map(
        dense_tile if small else by_slots,
        mesh=mesh,
        in_specs=in_specs,
        out_specs=out_specs,
        check_vma=False,
    )
```

```python
import functools

import jax
import jax.numpy as jnp
from jax import lax
from jax.experimental import pallas as pl
from jax.experimental.pallas import tpu as pltpu
from jax.sharding import PartitionSpec as P

F32 = jnp.float32
BF16 = jnp.bfloat16
ROWS = 4
COLS = 4
WHOLE = pl.BlockSpec(memory_space=pltpu.VMEM)
SCALARS = pl.BlockSpec(memory_space=pltpu.SMEM)
LIMIT = pltpu.CompilerParams(vmem_limit_bytes=16 * 2**20)
BIAS_ROWS = 16
GROUP = 8


def pick_rows(pick_index, live_mask, source_rows):
    source_count = source_rows.shape[0]
    onehot = (
        (pick_index[:, None] == jnp.arange(source_count, dtype=jnp.int32)[None, :])
        & live_mask[:, None]
    ).astype(jnp.bfloat16)
    chosen = jnp.dot(
        onehot, source_rows.reshape(source_count, -1), preferred_element_type=jnp.float32
    ).astype(jnp.bfloat16)
    return chosen.reshape((pick_index.shape[0],) + source_rows.shape[1:])


def slot_terms(values, pick_index, live_mask, source_rows, forward_pass):
    chosen = pick_rows(pick_index, live_mask, source_rows)
    if forward_pass:
        return jnp.einsum("spq,sqf->spf", values, chosen, preferred_element_type=jnp.float32)
    return jnp.einsum("spq,spf->sqf", values, chosen, preferred_element_type=jnp.float32)


def place_terms(products, place_index, blocks):
    block_ids = jnp.arange(blocks, dtype=jnp.int32)
    onehot = (block_ids[:, None] == place_index[None, :]).astype(jnp.bfloat16)
    flat = products.reshape(products.shape[0], -1)
    upper = flat.astype(jnp.bfloat16)
    lower = (flat - upper.astype(jnp.float32)).astype(jnp.bfloat16)
    placed = jnp.dot(onehot, upper, preferred_element_type=jnp.float32)
    placed = placed + jnp.dot(onehot, lower, preferred_element_type=jnp.float32)
    return placed.reshape(blocks * products.shape[1], products.shape[2])


def by_slots(features, block_values, block_rows, block_cols, block_count, weight, bias, cotangent):
    block_size = block_values.shape[1]
    slot_total = block_values.shape[0]
    live_mask = jnp.arange(slot_total, dtype=jnp.int32) < block_count[0]
    node_rows = cotangent.shape[0]
    width_in = features.shape[1]
    column_rows = lax.all_gather(features, "row", axis=0, tiled=True)
    column_blocks = column_rows.reshape(-1, block_size, width_in)
    forward_terms = slot_terms(block_values, block_cols, live_mask, column_blocks, True)
    aggregate = lax.psum_scatter(
        place_terms(
            forward_terms, block_rows, lax.axis_size("col") * node_rows // block_size
        ).astype(jnp.bfloat16),
        "col",
        scatter_dimension=0,
        tiled=True,
    ).astype(jnp.float32)
    aggregate = aggregate.astype(jnp.bfloat16)
    pre_act = jnp.dot(aggregate, weight, preferred_element_type=jnp.float32) + bias
    sigmoid_pre = jax.nn.sigmoid(pre_act)
    hidden = (pre_act * sigmoid_pre).astype(jnp.bfloat16)
    pre_grad = (
        cotangent.astype(jnp.float32) * sigmoid_pre * (1.0 + pre_act * (1.0 - sigmoid_pre))
    ).astype(jnp.bfloat16)
    grad_local = lax.dot_general(
        aggregate, pre_grad, (((0,), (0,)), ((), ())), preferred_element_type=jnp.float32
    )
    bias_local = jnp.sum(pre_grad.astype(jnp.float32), axis=0)
    grad_weight, grad_bias = lax.psum((grad_local, bias_local), ("row", "col"))
    norm_scale = float(node_rows * lax.axis_size("row") * lax.axis_size("col")) ** (-0.5)
    agg_grad = lax.dot_general(
        pre_grad, weight, (((1,), (1,)), ((), ())), preferred_element_type=jnp.float32
    ).astype(jnp.bfloat16)
    stripe_rows = lax.all_gather(agg_grad, "col", axis=0, tiled=True)
    stripe_blocks = stripe_rows.reshape(-1, block_size, width_in)
    backward_terms = slot_terms(block_values, block_rows, live_mask, stripe_blocks, False)
    grad_features = lax.psum_scatter(
        place_terms(
            backward_terms, block_cols, lax.axis_size("row") * node_rows // block_size
        ).astype(jnp.bfloat16),
        "row",
        scatter_dimension=0,
        tiled=True,
    )
    return (hidden, grad_weight * norm_scale, grad_bias * norm_scale, grad_features)


def densify_kernel(chunks, row_blocks, col_blocks, count_in, rows_in, cols_in, values_ref, tile_ref,
                   held, acc, count_ref, rows_ref, cols_ref, sems, scalar_sems):
    slots, block, _ = values_ref.shape
    size = slots // chunks
    scalars = [
        pltpu.make_async_copy(source, held_in, scalar_sems.at[i])
        for i, (source, held_in) in enumerate(
            ((count_in, count_ref), (rows_in, rows_ref), (cols_in, cols_ref))
        )
    ]
    copies = [
        pltpu.make_async_copy(
            values_ref.at[pl.ds(i * size, size)], held.at[pl.ds(i * size, size)], sems.at[i]
        )
        for i in range(chunks)
    ]
    for copy in scalars + copies:
        copy.start()
    acc[...] = jnp.zeros_like(acc)
    for copy in scalars:
        copy.wait()
    live = count_ref[0, 0]

    def add_slot(i, carry):
        place = rows_ref[i] * col_blocks + cols_ref[i]
        acc[place] = acc[place] + held[i].astype(F32)
        return carry

    def add_group(first, i, carry):
        for j in range(GROUP):
            add_slot(first + i * GROUP + j, carry)
        return carry

    for i, copy in enumerate(copies):
        copy.wait()
        here = jnp.clip(live - i * size, 0, size)
        groups = here // GROUP
        lax.fori_loop(0, groups, functools.partial(add_group, i * size), 0)
        lax.fori_loop(i * size + groups * GROUP, i * size + here, add_slot, 0)
    for r in range(row_blocks):
        for c in range(col_blocks):
            tile_ref[pl.ds(r * block, block), pl.ds(c * block, block)] = acc[
                r * col_blocks + c
            ].astype(BF16)


def densify(values, rows, cols, count, row_blocks, col_blocks):
    slots, block, _ = values.shape
    chunks = 8
    in_hbm = [
        pltpu.with_memory_space_constraint(array, pltpu.HBM)
        for array in (rows, cols, values)
    ]
    return pl.pallas_call(
        functools.partial(densify_kernel, chunks, row_blocks, col_blocks),
        in_specs=[WHOLE] + [pl.BlockSpec(memory_space=pltpu.HBM)] * 3,
        out_specs=WHOLE,
        out_shape=jax.ShapeDtypeStruct((row_blocks * block, col_blocks * block), BF16),
        scratch_shapes=[
            pltpu.VMEM(values.shape, BF16),
            pltpu.VMEM((row_blocks * col_blocks, block, block), F32),
            pltpu.SMEM((1, 1), jnp.int32),
            pltpu.SMEM(rows.shape, jnp.int32),
            pltpu.SMEM(cols.shape, jnp.int32),
            pltpu.SemaphoreType.DMA((chunks,)),
            pltpu.SemaphoreType.DMA((3,)),
        ],
        compiler_params=LIMIT,
        cost_estimate=pl.CostEstimate(flops=slots * block * block, bytes_accessed=values.size * 2, transcendentals=0),
        name="densify",
    )(count.reshape(1, 1), *in_hbm)


def forward_kernel(mine, tile_ref, outer_ref, x1, x2, out_ref):
    row = lax.axis_index("row")
    core = lax.rem(lax.axis_index("col"), 2)
    half = core if mine else 1 - core
    rows = x1.shape[0]
    for x in range(2):
        row_at = pl.multiple_of((2 * x + half) * rows, rows)
        total = None
        for k, shard in ((0, outer_ref[:rows, :]), (3, outer_ref[rows:, :]), (1, x1[...]), (2, x2[...])):
            col_at = pl.multiple_of(jnp.bitwise_xor(row, k) * rows, rows)
            tile = tile_ref[pl.ds(row_at, rows), pl.ds(col_at, rows)]
            term = jnp.dot(tile, shard, preferred_element_type=F32)
            total = term if total is None else total + term
        out_ref[pl.ds(x * rows, rows), :] = total.astype(out_ref.dtype)


def forward(mine, tile, outer, shards):
    rows, width_in = shards[0].shape
    return pl.pallas_call(
        functools.partial(forward_kernel, mine),
        in_specs=[WHOLE] * 4,
        out_specs=WHOLE,
        out_shape=jax.ShapeDtypeStruct((2 * rows, width_in), F32 if mine else BF16),
        compiler_params=LIMIT,
        cost_estimate=pl.CostEstimate(flops=tile.size * width_in, bytes_accessed=tile.size, transcendentals=0),
        name="forward_mine" if mine else "forward_sibling",
    )(tile, outer, *shards)


def layer_kernel(near_ref, far_ref, cot_ref, cot_far_ref, weight_ref, bias_ref, act_ref, swap_ref):
    mine = lax.rem(lax.axis_index("col") // 2, 2)
    rows, hid = cot_ref.shape
    width_in = near_ref.shape[1]
    weight = weight_ref[...]
    gw = None
    gb = None
    for x in range(2):
        block = pl.ds(x * rows, rows)
        aggregate = (near_ref[block, :].astype(F32) + far_ref[block, :].astype(F32)).astype(BF16)
        pre_act = jnp.dot(aggregate, weight, preferred_element_type=F32) + bias_ref[...]
        sigmoid_pre = jax.nn.sigmoid(pre_act)

        @pl.when(mine == x)
        def _():
            act_ref[...] = pre_act

        cot = jnp.where(mine == x, cot_ref[...], cot_far_ref[...]).astype(F32)
        pre_grad = (cot * sigmoid_pre * (1.0 + pre_act * (1.0 - sigmoid_pre))).astype(BF16)
        swap_ref[block, :] = lax.dot_general(
            pre_grad, weight, (((1,), (1,)), ((), ())), preferred_element_type=F32
        ).astype(BF16)
        term = lax.dot_general(
            aggregate, pre_grad, (((0,), (0,)), ((), ())), preferred_element_type=F32
        )
        bias_term = jnp.sum(pre_grad.astype(F32), axis=0, keepdims=True)
        gw = term if gw is None else gw + term
        gb = bias_term if gb is None else gb + bias_term
    at = 2 * rows
    for j in range(hid // width_in):
        lanes = slice(j * width_in, (j + 1) * width_in)
        swap_ref[pl.ds(at + j * width_in, width_in), :] = gw[:, lanes].astype(BF16)
    at = at + hid
    swap_ref[pl.ds(at, BIAS_ROWS), :] = jnp.concatenate(
        [gb[:, j * width_in : (j + 1) * width_in] for j in range(hid // width_in)]
        + [jnp.zeros((BIAS_ROWS - hid // width_in, width_in), F32)],
        axis=0,
    ).astype(BF16)


def backward_terms(tile_ref, half, k, grad_ref, rows):
    col_at = pl.multiple_of(jnp.bitwise_xor(lax.axis_index("row"), k) * rows, rows)
    total = None
    for x in range(2):
        row_at = pl.multiple_of((2 * x + half) * rows, rows)
        term = lax.dot_general(
            tile_ref[pl.ds(row_at, rows), pl.ds(col_at, rows)],
            grad_ref[pl.ds(x * rows, rows), :],
            (((0,), (0,)), ((), ())),
            preferred_element_type=F32,
        )
        total = term if total is None else total + term
    return total


def backward_mine_kernel(tile_ref, own_ref, part_ref):
    core = lax.rem(lax.axis_index("col"), 2)
    for k in range(ROWS):
        part_ref[k] = backward_terms(tile_ref, core, k, own_ref, part_ref.shape[1])


def backward_kernel(tile_ref, own_ref, sib_ref, part_ref, keep_ref, send1, send2, send3):
    core = lax.rem(lax.axis_index("col"), 2)
    rows = keep_ref.shape[0]
    for k, out in ((1, send1), (2, send2), (3, send3), (0, keep_ref)):
        total = part_ref[k] + backward_terms(tile_ref, 1 - core, k, sib_ref, rows)
        out[...] = total.astype(out.dtype)


def stripe_kernel(own_ref, sib_ref, stripe_ref):
    core = lax.rem(lax.axis_index("col"), 2)
    width_in = own_ref.shape[1]
    first = own_ref.shape[0] - BIAS_ROWS - 2 * width_in
    for source, target, size in (
        (pl.multiple_of(first + core * width_in, BIAS_ROWS), 0, width_in),
        (own_ref.shape[0] - BIAS_ROWS, width_in, BIAS_ROWS),
    ):
        stripe_ref[pl.ds(target, size), :] = (
            own_ref[pl.ds(source, size), :].astype(F32) + sib_ref[pl.ds(source, size), :].astype(F32)
        ).astype(BF16)


def last_kernel(scale, keep_ref, got1, got2, got3, pair_ref, pair_far_ref, half_ref, sib_ref,
                features_ref, gw_ref, gb_ref):
    core = lax.rem(lax.axis_index("col"), 2)
    width_in, hid = gw_ref.shape
    half = half_ref[...] * scale
    sib = sib_ref[...] * scale
    for j in range(2):
        gw_ref[:, j * width_in : (j + 1) * width_in] = jnp.where(core == j, half, sib)
    block = pl.ds(width_in, BIAS_ROWS)
    both = (pair_ref[block, :].astype(F32) + pair_far_ref[block, :].astype(F32)) * scale
    for j in range(hid // width_in):
        gb_ref[:, j * width_in : (j + 1) * width_in] = both[j : j + 1, :]
    total = keep_ref[...] + got1[...].astype(F32)
    total = total + got2[...].astype(F32) + got3[...].astype(F32)
    features_ref[...] = total.astype(BF16)


def swap(array, axis, bit):
    size = lax.axis_size(axis)
    return lax.ppermute(array, axis, [(i, i ^ bit) for i in range(size)])


def dense_tile(features, block_values, block_rows, block_cols, block_count, weight, bias, cotangent):
    block_size = block_values.shape[1]
    node_rows = cotangent.shape[0]
    width_in = features.shape[1]
    hid = cotangent.shape[1]
    row_blocks = COLS * node_rows // block_size
    col_blocks = ROWS * node_rows // block_size
    extra = hid + BIAS_ROWS
    shards = [swap(features, "row", k) for k in (1, 2)]
    outer = jnp.concatenate([features, swap(features, "row", 3)])
    tile = densify(block_values, block_rows, block_cols, block_count, row_blocks, col_blocks)
    cot_far = swap(cotangent, "col", 2)
    send = forward(False, tile, outer, shards)
    keep = forward(True, tile, outer, shards)
    sib, cot_far = lax.optimization_barrier((swap(send, "col", 1), cot_far))
    near = (keep + sib.astype(F32)).astype(BF16)
    far = swap(near, "col", 2)
    pre_act, grads = pl.pallas_call(
        layer_kernel,
        in_specs=[WHOLE] * 6,
        out_specs=[WHOLE] * 2,
        out_shape=[
            pltpu.VMEM((node_rows, hid), F32),
            jax.ShapeDtypeStruct((2 * node_rows + extra, width_in), BF16),
        ],
        compiler_params=LIMIT,
        name="layer",
    )(near, far, cotangent, cot_far, weight, bias.reshape(1, hid))
    block = jax.ShapeDtypeStruct((node_rows, width_in), BF16)
    part = pl.pallas_call(
        backward_mine_kernel,
        in_specs=[WHOLE] * 2,
        out_specs=WHOLE,
        out_shape=jax.ShapeDtypeStruct((ROWS, node_rows, width_in), F32),
        compiler_params=LIMIT,
        cost_estimate=pl.CostEstimate(flops=tile.size * width_in, bytes_accessed=tile.size, transcendentals=0),
        name="backward_mine",
    )(tile, grads)
    part, grads_sib = lax.optimization_barrier((part, swap(grads, "col", 1)))
    stripe = pl.pallas_call(
        stripe_kernel,
        in_specs=[WHOLE] * 2,
        out_specs=WHOLE,
        out_shape=jax.ShapeDtypeStruct((width_in + BIAS_ROWS, width_in), BF16),
        compiler_params=LIMIT,
        name="stripe",
    )(grads, grads_sib)
    stripe_far = swap(stripe, "row", 1)
    own, *sends = pl.pallas_call(
        backward_kernel,
        in_specs=[WHOLE] * 4,
        out_specs=[WHOLE] * 4,
        out_shape=[jax.ShapeDtypeStruct(block.shape, F32)] + [block] * 3,
        compiler_params=LIMIT,
        name="backward",
    )(tile, grads, grads_sib, part)
    pair = (stripe.astype(F32) + stripe_far.astype(F32)).astype(BF16)
    pair, sends[2] = lax.optimization_barrier((pair, sends[2]))
    got = [swap(send, "row", k) for k, send in zip((1, 2, 3), sends)]
    pair, pre_act = lax.optimization_barrier((pair, pre_act))
    hidden = (pre_act * jax.nn.sigmoid(pre_act)).astype(BF16)
    pair_far = swap(pair, "row", 2)
    gw_half = pair[:width_in].astype(F32) + pair_far[:width_in].astype(F32)
    gw_half, hidden = lax.optimization_barrier((gw_half, hidden))
    gw_sib = swap(gw_half, "col", 1)
    norm_scale = float(node_rows * ROWS * COLS) ** (-0.5)
    grad_features, grad_weight, grad_bias = pl.pallas_call(
        functools.partial(last_kernel, norm_scale),
        in_specs=[WHOLE] * 8,
        out_specs=[WHOLE] * 3,
        out_shape=[
            block,
            jax.ShapeDtypeStruct((width_in, hid), F32),
            jax.ShapeDtypeStruct((1, hid), F32),
        ],
        compiler_params=LIMIT,
        name="last",
    )(own, *got, pair, pair_far, gw_half, gw_sib)
    return hidden, grad_weight, grad_bias.reshape(hid), grad_features


def solution(mesh):
    in_specs = (
        P(("parts", "col", "row"), None),
        P(("parts", "row", "col"), None, None),
        P(("parts", "row", "col")),
        P(("parts", "row", "col")),
        P(("parts", "row", "col")),
        P(),
        P(),
        P(("parts", "row", "col"), None),
    )
    out_specs = (
        P(("parts", "row", "col"), None),
        P("parts", None),
        P("parts"),
        P(("parts", "col", "row"), None),
    )
    small = mesh.shape["row"] == ROWS and mesh.shape["col"] == COLS
    return jax.shard_map(
        dense_tile if small else by_slots,
        mesh=mesh,
        in_specs=in_specs,
        out_specs=out_specs,
        check_vma=False,
    )
```

```python
import functools

import jax
import jax.numpy as jnp
from jax import lax
from jax.experimental import pallas as pl
from jax.experimental.pallas import tpu as pltpu
from jax.sharding import PartitionSpec as P

F32 = jnp.float32
BF16 = jnp.bfloat16
ROWS = 4
COLS = 4
WHOLE = pl.BlockSpec(memory_space=pltpu.VMEM)
SCALARS = pl.BlockSpec(memory_space=pltpu.SMEM)
LIMIT = pltpu.CompilerParams(vmem_limit_bytes=16 * 2**20)
BIAS_ROWS = 16
GROUP = 8


def pick_rows(pick_index, live_mask, source_rows):
    source_count = source_rows.shape[0]
    onehot = (
        (pick_index[:, None] == jnp.arange(source_count, dtype=jnp.int32)[None, :])
        & live_mask[:, None]
    ).astype(jnp.bfloat16)
    chosen = jnp.dot(
        onehot, source_rows.reshape(source_count, -1), preferred_element_type=jnp.float32
    ).astype(jnp.bfloat16)
    return chosen.reshape((pick_index.shape[0],) + source_rows.shape[1:])


def slot_terms(values, pick_index, live_mask, source_rows, forward_pass):
    chosen = pick_rows(pick_index, live_mask, source_rows)
    if forward_pass:
        return jnp.einsum("spq,sqf->spf", values, chosen, preferred_element_type=jnp.float32)
    return jnp.einsum("spq,spf->sqf", values, chosen, preferred_element_type=jnp.float32)


def place_terms(products, place_index, blocks):
    block_ids = jnp.arange(blocks, dtype=jnp.int32)
    onehot = (block_ids[:, None] == place_index[None, :]).astype(jnp.bfloat16)
    flat = products.reshape(products.shape[0], -1)
    upper = flat.astype(jnp.bfloat16)
    lower = (flat - upper.astype(jnp.float32)).astype(jnp.bfloat16)
    placed = jnp.dot(onehot, upper, preferred_element_type=jnp.float32)
    placed = placed + jnp.dot(onehot, lower, preferred_element_type=jnp.float32)
    return placed.reshape(blocks * products.shape[1], products.shape[2])


def by_slots(features, block_values, block_rows, block_cols, block_count, weight, bias, cotangent):
    block_size = block_values.shape[1]
    slot_total = block_values.shape[0]
    live_mask = jnp.arange(slot_total, dtype=jnp.int32) < block_count[0]
    node_rows = cotangent.shape[0]
    width_in = features.shape[1]
    column_rows = lax.all_gather(features, "row", axis=0, tiled=True)
    column_blocks = column_rows.reshape(-1, block_size, width_in)
    forward_terms = slot_terms(block_values, block_cols, live_mask, column_blocks, True)
    aggregate = lax.psum_scatter(
        place_terms(
            forward_terms, block_rows, lax.axis_size("col") * node_rows // block_size
        ).astype(jnp.bfloat16),
        "col",
        scatter_dimension=0,
        tiled=True,
    ).astype(jnp.float32)
    aggregate = aggregate.astype(jnp.bfloat16)
    pre_act = jnp.dot(aggregate, weight, preferred_element_type=jnp.float32) + bias
    sigmoid_pre = jax.nn.sigmoid(pre_act)
    hidden = (pre_act * sigmoid_pre).astype(jnp.bfloat16)
    pre_grad = (
        cotangent.astype(jnp.float32) * sigmoid_pre * (1.0 + pre_act * (1.0 - sigmoid_pre))
    ).astype(jnp.bfloat16)
    grad_local = lax.dot_general(
        aggregate, pre_grad, (((0,), (0,)), ((), ())), preferred_element_type=jnp.float32
    )
    bias_local = jnp.sum(pre_grad.astype(jnp.float32), axis=0)
    grad_weight, grad_bias = lax.psum((grad_local, bias_local), ("row", "col"))
    norm_scale = float(node_rows * lax.axis_size("row") * lax.axis_size("col")) ** (-0.5)
    agg_grad = lax.dot_general(
        pre_grad, weight, (((1,), (1,)), ((), ())), preferred_element_type=jnp.float32
    ).astype(jnp.bfloat16)
    stripe_rows = lax.all_gather(agg_grad, "col", axis=0, tiled=True)
    stripe_blocks = stripe_rows.reshape(-1, block_size, width_in)
    backward_terms = slot_terms(block_values, block_rows, live_mask, stripe_blocks, False)
    grad_features = lax.psum_scatter(
        place_terms(
            backward_terms, block_cols, lax.axis_size("row") * node_rows // block_size
        ).astype(jnp.bfloat16),
        "row",
        scatter_dimension=0,
        tiled=True,
    )
    return (hidden, grad_weight * norm_scale, grad_bias * norm_scale, grad_features)


def densify_kernel(chunks, row_blocks, col_blocks, count_in, rows_in, cols_in, values_ref, tile_ref,
                   held, acc, count_ref, rows_ref, cols_ref, sems, scalar_sems):
    slots, block, _ = values_ref.shape
    size = slots // chunks
    scalars = [
        pltpu.make_async_copy(source, held_in, scalar_sems.at[i])
        for i, (source, held_in) in enumerate(
            ((count_in, count_ref), (rows_in, rows_ref), (cols_in, cols_ref))
        )
    ]
    copies = [
        pltpu.make_async_copy(
            values_ref.at[pl.ds(i * size, size)], held.at[pl.ds(i * size, size)], sems.at[i]
        )
        for i in range(chunks)
    ]
    for copy in scalars + copies:
        copy.start()
    acc[...] = jnp.zeros_like(acc)
    for copy in scalars:
        copy.wait()
    live = count_ref[0, 0]

    def add_slot(i, carry):
        place = rows_ref[i] * col_blocks + cols_ref[i]
        acc[place] = acc[place] + held[i].astype(F32)
        return carry

    def add_group(first, i, carry):
        for j in range(GROUP):
            add_slot(first + i * GROUP + j, carry)
        return carry

    for i, copy in enumerate(copies):
        copy.wait()
        here = jnp.clip(live - i * size, 0, size)
        groups = here // GROUP
        lax.fori_loop(0, groups, functools.partial(add_group, i * size), 0)
        lax.fori_loop(i * size + groups * GROUP, i * size + here, add_slot, 0)
    for r in range(row_blocks):
        for c in range(col_blocks):
            tile_ref[pl.ds(r * block, block), pl.ds(c * block, block)] = acc[
                r * col_blocks + c
            ].astype(BF16)


def densify(values, rows, cols, count, row_blocks, col_blocks):
    slots, block, _ = values.shape
    chunks = 8
    in_hbm = [
        pltpu.with_memory_space_constraint(array, pltpu.HBM)
        for array in (rows, cols, values)
    ]
    return pl.pallas_call(
        functools.partial(densify_kernel, chunks, row_blocks, col_blocks),
        in_specs=[WHOLE] + [pl.BlockSpec(memory_space=pltpu.HBM)] * 3,
        out_specs=WHOLE,
        out_shape=jax.ShapeDtypeStruct((row_blocks * block, col_blocks * block), BF16),
        scratch_shapes=[
            pltpu.VMEM(values.shape, BF16),
            pltpu.VMEM((row_blocks * col_blocks, block, block), F32),
            pltpu.SMEM((1, 1), jnp.int32),
            pltpu.SMEM(rows.shape, jnp.int32),
            pltpu.SMEM(cols.shape, jnp.int32),
            pltpu.SemaphoreType.DMA((chunks,)),
            pltpu.SemaphoreType.DMA((3,)),
        ],
        compiler_params=LIMIT,
        cost_estimate=pl.CostEstimate(flops=slots * block * block, bytes_accessed=values.size * 2, transcendentals=0),
        name="densify",
    )(count.reshape(1, 1), *in_hbm)


def forward_kernel(mine, tile_ref, outer_ref, x1, x2, out_ref):
    row = lax.axis_index("row")
    core = lax.rem(lax.axis_index("col"), 2)
    half = core if mine else 1 - core
    rows = x1.shape[0]
    for x in range(2):
        row_at = pl.multiple_of((2 * x + half) * rows, rows)
        total = None
        for k, shard in ((0, outer_ref[:rows, :]), (3, outer_ref[rows:, :]), (1, x1[...]), (2, x2[...])):
            col_at = pl.multiple_of(jnp.bitwise_xor(row, k) * rows, rows)
            tile = tile_ref[pl.ds(row_at, rows), pl.ds(col_at, rows)]
            term = jnp.dot(tile, shard, preferred_element_type=F32)
            total = term if total is None else total + term
        out_ref[pl.ds(x * rows, rows), :] = total.astype(out_ref.dtype)


def forward(mine, tile, outer, shards):
    rows, width_in = shards[0].shape
    return pl.pallas_call(
        functools.partial(forward_kernel, mine),
        in_specs=[WHOLE] * 4,
        out_specs=WHOLE,
        out_shape=jax.ShapeDtypeStruct((2 * rows, width_in), F32 if mine else BF16),
        compiler_params=LIMIT,
        cost_estimate=pl.CostEstimate(flops=tile.size * width_in, bytes_accessed=tile.size, transcendentals=0),
        name="forward_mine" if mine else "forward_sibling",
    )(tile, outer, *shards)


def layer_kernel(near_ref, far_ref, cot_ref, cot_far_ref, weight_ref, bias_ref, act_ref, swap_ref):
    mine = lax.rem(lax.axis_index("col") // 2, 2)
    rows, hid = cot_ref.shape
    width_in = near_ref.shape[1]
    weight = weight_ref[...]
    gw = None
    gb = None
    for x in range(2):
        block = pl.ds(x * rows, rows)
        aggregate = (near_ref[block, :].astype(F32) + far_ref[block, :].astype(F32)).astype(BF16)
        pre_act = jnp.dot(aggregate, weight, preferred_element_type=F32) + bias_ref[...]
        sigmoid_pre = jax.nn.sigmoid(pre_act)

        @pl.when(mine == x)
        def _():
            act_ref[...] = pre_act

        cot = jnp.where(mine == x, cot_ref[...], cot_far_ref[...]).astype(F32)
        pre_grad = (cot * sigmoid_pre * (1.0 + pre_act * (1.0 - sigmoid_pre))).astype(BF16)
        swap_ref[block, :] = lax.dot_general(
            pre_grad, weight, (((1,), (1,)), ((), ())), preferred_element_type=F32
        ).astype(BF16)
        term = lax.dot_general(
            aggregate, pre_grad, (((0,), (0,)), ((), ())), preferred_element_type=F32
        )
        bias_term = jnp.sum(pre_grad.astype(F32), axis=0, keepdims=True)
        gw = term if gw is None else gw + term
        gb = bias_term if gb is None else gb + bias_term
    at = 2 * rows
    for j in range(hid // width_in):
        lanes = slice(j * width_in, (j + 1) * width_in)
        swap_ref[pl.ds(at + j * width_in, width_in), :] = gw[:, lanes].astype(BF16)
    at = at + hid
    swap_ref[pl.ds(at, BIAS_ROWS), :] = jnp.concatenate(
        [gb[:, j * width_in : (j + 1) * width_in] for j in range(hid // width_in)]
        + [jnp.zeros((BIAS_ROWS - hid // width_in, width_in), F32)],
        axis=0,
    ).astype(BF16)


def backward_terms(tile_ref, half, k, grad_ref, rows):
    col_at = pl.multiple_of(jnp.bitwise_xor(lax.axis_index("row"), k) * rows, rows)
    total = None
    for x in range(2):
        row_at = pl.multiple_of((2 * x + half) * rows, rows)
        term = lax.dot_general(
            tile_ref[pl.ds(row_at, rows), pl.ds(col_at, rows)],
            grad_ref[pl.ds(x * rows, rows), :],
            (((0,), (0,)), ((), ())),
            preferred_element_type=F32,
        )
        total = term if total is None else total + term
    return total


def backward_mine_kernel(tile_ref, own_ref, part_ref):
    core = lax.rem(lax.axis_index("col"), 2)
    for k in range(ROWS):
        part_ref[k] = backward_terms(tile_ref, core, k, own_ref, part_ref.shape[1])


def backward_kernel(tile_ref, own_ref, sib_ref, part_ref, keep_ref, send1, send2, send3):
    core = lax.rem(lax.axis_index("col"), 2)
    rows = keep_ref.shape[0]
    for k, out in ((1, send1), (2, send2), (3, send3), (0, keep_ref)):
        total = part_ref[k] + backward_terms(tile_ref, 1 - core, k, sib_ref, rows)
        out[...] = total.astype(out.dtype)


def stripe_kernel(own_ref, sib_ref, stripe_ref):
    core = lax.rem(lax.axis_index("col"), 2)
    width_in = own_ref.shape[1]
    first = own_ref.shape[0] - BIAS_ROWS - 2 * width_in
    for source, target, size in (
        (pl.multiple_of(first + core * width_in, BIAS_ROWS), 0, width_in),
        (own_ref.shape[0] - BIAS_ROWS, width_in, BIAS_ROWS),
    ):
        stripe_ref[pl.ds(target, size), :] = (
            own_ref[pl.ds(source, size), :].astype(F32) + sib_ref[pl.ds(source, size), :].astype(F32)
        ).astype(BF16)


def last_kernel(scale, keep_ref, got1, got2, got3, act_ref, pair_ref, pair_far_ref, half_ref, sib_ref,
                features_ref, hidden_ref, gw_ref, gb_ref):
    core = lax.rem(lax.axis_index("col"), 2)
    width_in, hid = gw_ref.shape
    half = half_ref[...] * scale
    sib = sib_ref[...] * scale
    for j in range(2):
        gw_ref[:, j * width_in : (j + 1) * width_in] = jnp.where(core == j, half, sib)
    block = pl.ds(width_in, BIAS_ROWS)
    both = (pair_ref[block, :].astype(F32) + pair_far_ref[block, :].astype(F32)) * scale
    for j in range(hid // width_in):
        gb_ref[:, j * width_in : (j + 1) * width_in] = both[j : j + 1, :]
    total = keep_ref[...] + got1[...].astype(F32)
    total = total + got2[...].astype(F32) + got3[...].astype(F32)
    features_ref[...] = total.astype(BF16)
    hidden_ref[...] = act_ref[...]


def swap(array, axis, bit):
    size = lax.axis_size(axis)
    return lax.ppermute(array, axis, [(i, i ^ bit) for i in range(size)])


def dense_tile(features, block_values, block_rows, block_cols, block_count, weight, bias, cotangent):
    block_size = block_values.shape[1]
    node_rows = cotangent.shape[0]
    width_in = features.shape[1]
    hid = cotangent.shape[1]
    row_blocks = COLS * node_rows // block_size
    col_blocks = ROWS * node_rows // block_size
    extra = hid + BIAS_ROWS
    shards = [swap(features, "row", k) for k in (1, 2)]
    outer = jnp.concatenate([features, swap(features, "row", 3)])
    tile = densify(block_values, block_rows, block_cols, block_count, row_blocks, col_blocks)
    cot_far = swap(cotangent, "col", 2)
    send = forward(False, tile, outer, shards)
    keep = forward(True, tile, outer, shards)
    sib, cot_far = lax.optimization_barrier((swap(send, "col", 1), cot_far))
    near = (keep + sib.astype(F32)).astype(BF16)
    far = swap(near, "col", 2)
    pre_act, grads = pl.pallas_call(
        layer_kernel,
        in_specs=[WHOLE] * 6,
        out_specs=[WHOLE] * 2,
        out_shape=[
            pltpu.VMEM((node_rows, hid), F32),
            jax.ShapeDtypeStruct((2 * node_rows + extra, width_in), BF16),
        ],
        compiler_params=LIMIT,
        name="layer",
    )(near, far, cotangent, cot_far, weight, bias.reshape(1, hid))
    block = jax.ShapeDtypeStruct((node_rows, width_in), BF16)
    part = pl.pallas_call(
        backward_mine_kernel,
        in_specs=[WHOLE] * 2,
        out_specs=WHOLE,
        out_shape=jax.ShapeDtypeStruct((ROWS, node_rows, width_in), F32),
        compiler_params=LIMIT,
        cost_estimate=pl.CostEstimate(flops=tile.size * width_in, bytes_accessed=tile.size, transcendentals=0),
        name="backward_mine",
    )(tile, grads)
    part, grads_sib = lax.optimization_barrier((part, swap(grads, "col", 1)))
    stripe = pl.pallas_call(
        stripe_kernel,
        in_specs=[WHOLE] * 2,
        out_specs=WHOLE,
        out_shape=jax.ShapeDtypeStruct((width_in + BIAS_ROWS, width_in), BF16),
        compiler_params=LIMIT,
        name="stripe",
    )(grads, grads_sib)
    stripe_far = swap(stripe, "row", 2)
    own, *sends = pl.pallas_call(
        backward_kernel,
        in_specs=[WHOLE] * 4,
        out_specs=[WHOLE] * 4,
        out_shape=[jax.ShapeDtypeStruct(block.shape, F32)] + [block] * 3,
        compiler_params=LIMIT,
        name="backward",
    )(tile, grads, grads_sib, part)
    pair = (stripe.astype(F32) + stripe_far.astype(F32)).astype(BF16)
    pair, sends[2] = lax.optimization_barrier((pair, sends[2]))
    got = [swap(send, "row", k) for k, send in zip((1, 2, 3), sends)]
    pair, pre_act = lax.optimization_barrier((pair, pre_act))
    hidden = (pre_act * jax.nn.sigmoid(pre_act)).astype(BF16)
    pair_far = swap(pair, "row", 1)
    gw_half = pair[:width_in].astype(F32) + pair_far[:width_in].astype(F32)
    gw_half, hidden = lax.optimization_barrier((gw_half, hidden))
    gw_sib = swap(gw_half, "col", 1)
    norm_scale = float(node_rows * ROWS * COLS) ** (-0.5)
    grad_features, hidden, grad_weight, grad_bias = pl.pallas_call(
        functools.partial(last_kernel, norm_scale),
        in_specs=[WHOLE] * 9,
        out_specs=[WHOLE] * 4,
        out_shape=[
            block,
            jax.ShapeDtypeStruct(hidden.shape, BF16),
            jax.ShapeDtypeStruct((width_in, hid), F32),
            jax.ShapeDtypeStruct((1, hid), F32),
        ],
        compiler_params=LIMIT,
        name="last",
    )(own, *got, hidden, pair, pair_far, gw_half, gw_sib)
    return hidden, grad_weight, grad_bias.reshape(hid), grad_features


def solution(mesh):
    in_specs = (
        P(("parts", "col", "row"), None),
        P(("parts", "row", "col"), None, None),
        P(("parts", "row", "col")),
        P(("parts", "row", "col")),
        P(("parts", "row", "col")),
        P(),
        P(),
        P(("parts", "row", "col"), None),
    )
    out_specs = (
        P(("parts", "row", "col"), None),
        P("parts", None),
        P("parts"),
        P(("parts", "col", "row"), None),
    )
    small = mesh.shape["row"] == ROWS and mesh.shape["col"] == COLS
    return jax.shard_map(
        dense_tile if small else by_slots,
        mesh=mesh,
        in_specs=in_specs,
        out_specs=out_specs,
        check_vma=False,
    )
```

```python
import functools

import jax
import jax.numpy as jnp
from jax import lax
from jax.experimental import pallas as pl
from jax.experimental.pallas import tpu as pltpu
from jax.sharding import PartitionSpec as P

F32 = jnp.float32
BF16 = jnp.bfloat16
ROWS = 4
COLS = 4
WHOLE = pl.BlockSpec(memory_space=pltpu.VMEM)
SCALARS = pl.BlockSpec(memory_space=pltpu.SMEM)
LIMIT = pltpu.CompilerParams(vmem_limit_bytes=16 * 2**20)
BIAS_ROWS = 16
GROUP = 8


def pick_rows(pick_index, live_mask, source_rows):
    source_count = source_rows.shape[0]
    onehot = (
        (pick_index[:, None] == jnp.arange(source_count, dtype=jnp.int32)[None, :])
        & live_mask[:, None]
    ).astype(jnp.bfloat16)
    chosen = jnp.dot(
        onehot, source_rows.reshape(source_count, -1), preferred_element_type=jnp.float32
    ).astype(jnp.bfloat16)
    return chosen.reshape((pick_index.shape[0],) + source_rows.shape[1:])


def slot_terms(values, pick_index, live_mask, source_rows, forward_pass):
    chosen = pick_rows(pick_index, live_mask, source_rows)
    if forward_pass:
        return jnp.einsum("spq,sqf->spf", values, chosen, preferred_element_type=jnp.float32)
    return jnp.einsum("spq,spf->sqf", values, chosen, preferred_element_type=jnp.float32)


def place_terms(products, place_index, blocks):
    block_ids = jnp.arange(blocks, dtype=jnp.int32)
    onehot = (block_ids[:, None] == place_index[None, :]).astype(jnp.bfloat16)
    flat = products.reshape(products.shape[0], -1)
    upper = flat.astype(jnp.bfloat16)
    lower = (flat - upper.astype(jnp.float32)).astype(jnp.bfloat16)
    placed = jnp.dot(onehot, upper, preferred_element_type=jnp.float32)
    placed = placed + jnp.dot(onehot, lower, preferred_element_type=jnp.float32)
    return placed.reshape(blocks * products.shape[1], products.shape[2])


def by_slots(features, block_values, block_rows, block_cols, block_count, weight, bias, cotangent):
    block_size = block_values.shape[1]
    slot_total = block_values.shape[0]
    live_mask = jnp.arange(slot_total, dtype=jnp.int32) < block_count[0]
    node_rows = cotangent.shape[0]
    width_in = features.shape[1]
    column_rows = lax.all_gather(features, "row", axis=0, tiled=True)
    column_blocks = column_rows.reshape(-1, block_size, width_in)
    forward_terms = slot_terms(block_values, block_cols, live_mask, column_blocks, True)
    aggregate = lax.psum_scatter(
        place_terms(
            forward_terms, block_rows, lax.axis_size("col") * node_rows // block_size
        ).astype(jnp.bfloat16),
        "col",
        scatter_dimension=0,
        tiled=True,
    ).astype(jnp.float32)
    aggregate = aggregate.astype(jnp.bfloat16)
    pre_act = jnp.dot(aggregate, weight, preferred_element_type=jnp.float32) + bias
    sigmoid_pre = jax.nn.sigmoid(pre_act)
    hidden = (pre_act * sigmoid_pre).astype(jnp.bfloat16)
    pre_grad = (
        cotangent.astype(jnp.float32) * sigmoid_pre * (1.0 + pre_act * (1.0 - sigmoid_pre))
    ).astype(jnp.bfloat16)
    grad_local = lax.dot_general(
        aggregate, pre_grad, (((0,), (0,)), ((), ())), preferred_element_type=jnp.float32
    )
    bias_local = jnp.sum(pre_grad.astype(jnp.float32), axis=0)
    grad_weight, grad_bias = lax.psum((grad_local, bias_local), ("row", "col"))
    norm_scale = float(node_rows * lax.axis_size("row") * lax.axis_size("col")) ** (-0.5)
    agg_grad = lax.dot_general(
        pre_grad, weight, (((1,), (1,)), ((), ())), preferred_element_type=jnp.float32
    ).astype(jnp.bfloat16)
    stripe_rows = lax.all_gather(agg_grad, "col", axis=0, tiled=True)
    stripe_blocks = stripe_rows.reshape(-1, block_size, width_in)
    backward_terms = slot_terms(block_values, block_rows, live_mask, stripe_blocks, False)
    grad_features = lax.psum_scatter(
        place_terms(
            backward_terms, block_cols, lax.axis_size("row") * node_rows // block_size
        ).astype(jnp.bfloat16),
        "row",
        scatter_dimension=0,
        tiled=True,
    )
    return (hidden, grad_weight * norm_scale, grad_bias * norm_scale, grad_features)


def densify_kernel(chunks, row_blocks, col_blocks, count_in, rows_in, cols_in, values_ref, tile_ref,
                   held, acc, count_ref, rows_ref, cols_ref, sems, scalar_sems):
    slots, block, _ = values_ref.shape
    size = slots // chunks
    scalars = [
        pltpu.make_async_copy(source, held_in, scalar_sems.at[i])
        for i, (source, held_in) in enumerate(
            ((count_in, count_ref), (rows_in, rows_ref), (cols_in, cols_ref))
        )
    ]
    copies = [
        pltpu.make_async_copy(
            values_ref.at[pl.ds(i * size, size)], held.at[pl.ds(i * size, size)], sems.at[i]
        )
        for i in range(chunks)
    ]
    for copy in scalars + copies:
        copy.start()
    acc[...] = jnp.zeros_like(acc)
    for copy in scalars:
        copy.wait()
    live = count_ref[0, 0]

    def add_slot(i, carry):
        place = rows_ref[i] * col_blocks + cols_ref[i]
        acc[place] = acc[place] + held[i].astype(F32)
        return carry

    def add_group(first, i, carry):
        for j in range(GROUP):
            add_slot(first + i * GROUP + j, carry)
        return carry

    for i, copy in enumerate(copies):
        copy.wait()
        here = jnp.clip(live - i * size, 0, size)
        groups = here // GROUP
        lax.fori_loop(0, groups, functools.partial(add_group, i * size), 0)
        lax.fori_loop(i * size + groups * GROUP, i * size + here, add_slot, 0)
    for r in range(row_blocks):
        for c in range(col_blocks):
            tile_ref[pl.ds(r * block, block), pl.ds(c * block, block)] = acc[
                r * col_blocks + c
            ].astype(BF16)


def densify(values, rows, cols, count, row_blocks, col_blocks):
    slots, block, _ = values.shape
    chunks = 8
    in_hbm = [
        pltpu.with_memory_space_constraint(array, pltpu.HBM)
        for array in (rows, cols, values)
    ]
    return pl.pallas_call(
        functools.partial(densify_kernel, chunks, row_blocks, col_blocks),
        in_specs=[WHOLE] + [pl.BlockSpec(memory_space=pltpu.HBM)] * 3,
        out_specs=WHOLE,
        out_shape=jax.ShapeDtypeStruct((row_blocks * block, col_blocks * block), BF16),
        scratch_shapes=[
            pltpu.VMEM(values.shape, BF16),
            pltpu.VMEM((row_blocks * col_blocks, block, block), F32),
            pltpu.SMEM((1, 1), jnp.int32),
            pltpu.SMEM(rows.shape, jnp.int32),
            pltpu.SMEM(cols.shape, jnp.int32),
            pltpu.SemaphoreType.DMA((chunks,)),
            pltpu.SemaphoreType.DMA((3,)),
        ],
        compiler_params=LIMIT,
        cost_estimate=pl.CostEstimate(flops=slots * block * block, bytes_accessed=values.size * 2, transcendentals=0),
        name="densify",
    )(count.reshape(1, 1), *in_hbm)


def forward_kernel(mine, tile_ref, outer_ref, x1, x2, out_ref):
    row = lax.axis_index("row")
    core = lax.rem(lax.axis_index("col"), 2)
    half = core if mine else 1 - core
    rows = x1.shape[0]
    for x in range(2):
        row_at = pl.multiple_of((2 * x + half) * rows, rows)
        total = None
        for k, shard in ((0, outer_ref[:rows, :]), (3, outer_ref[rows:, :]), (1, x1[...]), (2, x2[...])):
            col_at = pl.multiple_of(jnp.bitwise_xor(row, k) * rows, rows)
            tile = tile_ref[pl.ds(row_at, rows), pl.ds(col_at, rows)]
            term = jnp.dot(tile, shard, preferred_element_type=F32)
            total = term if total is None else total + term
        out_ref[pl.ds(x * rows, rows), :] = total.astype(out_ref.dtype)


def forward(mine, tile, outer, shards):
    rows, width_in = shards[0].shape
    return pl.pallas_call(
        functools.partial(forward_kernel, mine),
        in_specs=[WHOLE] * 4,
        out_specs=WHOLE,
        out_shape=jax.ShapeDtypeStruct((2 * rows, width_in), F32 if mine else BF16),
        compiler_params=LIMIT,
        cost_estimate=pl.CostEstimate(flops=tile.size * width_in, bytes_accessed=tile.size, transcendentals=0),
        name="forward_mine" if mine else "forward_sibling",
    )(tile, outer, *shards)


def layer_kernel(near_ref, far_ref, cot_ref, cot_far_ref, weight_ref, bias_ref, act_ref, swap_ref):
    mine = lax.rem(lax.axis_index("col") // 2, 2)
    rows, hid = cot_ref.shape
    width_in = near_ref.shape[1]
    weight = weight_ref[...]
    gw = None
    gb = None
    for other, source_ref in enumerate((cot_ref, cot_far_ref)):
        block = pl.ds(pl.multiple_of(jnp.bitwise_xor(mine, other) * rows, rows), rows)
        aggregate = (near_ref[block, :].astype(F32) + far_ref[block, :].astype(F32)).astype(BF16)
        pre_act = jnp.dot(aggregate, weight, preferred_element_type=F32) + bias_ref[...]
        sigmoid_pre = jax.nn.sigmoid(pre_act)
        if other == 0:
            act_ref[...] = pre_act
        cot = source_ref[...].astype(F32)
        pre_grad = (cot * sigmoid_pre * (1.0 + pre_act * (1.0 - sigmoid_pre))).astype(BF16)
        swap_ref[block, :] = lax.dot_general(
            pre_grad, weight, (((1,), (1,)), ((), ())), preferred_element_type=F32
        ).astype(BF16)
        term = lax.dot_general(
            aggregate, pre_grad, (((0,), (0,)), ((), ())), preferred_element_type=F32
        )
        bias_term = jnp.sum(pre_grad.astype(F32), axis=0, keepdims=True)
        gw = term if gw is None else gw + term
        gb = bias_term if gb is None else gb + bias_term
    at = 2 * rows
    for j in range(hid // width_in):
        lanes = slice(j * width_in, (j + 1) * width_in)
        swap_ref[pl.ds(at + j * width_in, width_in), :] = gw[:, lanes].astype(BF16)
    at = at + hid
    swap_ref[pl.ds(at, BIAS_ROWS), :] = jnp.concatenate(
        [gb[:, j * width_in : (j + 1) * width_in] for j in range(hid // width_in)]
        + [jnp.zeros((BIAS_ROWS - hid // width_in, width_in), F32)],
        axis=0,
    ).astype(BF16)


def backward_terms(tile_ref, half, k, grad_ref, rows):
    col_at = pl.multiple_of(jnp.bitwise_xor(lax.axis_index("row"), k) * rows, rows)
    total = None
    for x in range(2):
        row_at = pl.multiple_of((2 * x + half) * rows, rows)
        term = lax.dot_general(
            tile_ref[pl.ds(row_at, rows), pl.ds(col_at, rows)],
            grad_ref[pl.ds(x * rows, rows), :],
            (((0,), (0,)), ((), ())),
            preferred_element_type=F32,
        )
        total = term if total is None else total + term
    return total


def backward_mine_kernel(tile_ref, own_ref, part_ref):
    core = lax.rem(lax.axis_index("col"), 2)
    for k in range(ROWS):
        part_ref[k] = backward_terms(tile_ref, core, k, own_ref, part_ref.shape[1])


def backward_kernel(tile_ref, own_ref, sib_ref, part_ref, keep_ref, send1, send2, send3):
    core = lax.rem(lax.axis_index("col"), 2)
    rows = keep_ref.shape[0]
    for k, out in ((1, send1), (2, send2), (3, send3), (0, keep_ref)):
        total = part_ref[k] + backward_terms(tile_ref, 1 - core, k, sib_ref, rows)
        out[...] = total.astype(out.dtype)


def stripe_kernel(own_ref, sib_ref, stripe_ref):
    core = lax.rem(lax.axis_index("col"), 2)
    width_in = own_ref.shape[1]
    first = own_ref.shape[0] - BIAS_ROWS - 2 * width_in
    for source, target, size in (
        (pl.multiple_of(first + core * width_in, BIAS_ROWS), 0, width_in),
        (own_ref.shape[0] - BIAS_ROWS, width_in, BIAS_ROWS),
    ):
        stripe_ref[pl.ds(target, size), :] = (
            own_ref[pl.ds(source, size), :].astype(F32) + sib_ref[pl.ds(source, size), :].astype(F32)
        ).astype(BF16)


def last_kernel(scale, keep_ref, got1, got2, got3, act_ref, pair_ref, pair_far_ref, half_ref, sib_ref,
                features_ref, hidden_ref, gw_ref, gb_ref):
    core = lax.rem(lax.axis_index("col"), 2)
    width_in, hid = gw_ref.shape
    half = half_ref[...] * scale
    sib = sib_ref[...] * scale
    for j in range(2):
        gw_ref[:, j * width_in : (j + 1) * width_in] = jnp.where(core == j, half, sib)
    block = pl.ds(width_in, BIAS_ROWS)
    both = (pair_ref[block, :].astype(F32) + pair_far_ref[block, :].astype(F32)) * scale
    for j in range(hid // width_in):
        gb_ref[:, j * width_in : (j + 1) * width_in] = both[j : j + 1, :]
    total = keep_ref[...] + got1[...].astype(F32)
    total = total + got2[...].astype(F32) + got3[...].astype(F32)
    features_ref[...] = total.astype(BF16)
    hidden_ref[...] = act_ref[...]


def swap(array, axis, bit):
    size = lax.axis_size(axis)
    return lax.ppermute(array, axis, [(i, i ^ bit) for i in range(size)])


def dense_tile(features, block_values, block_rows, block_cols, block_count, weight, bias, cotangent):
    block_size = block_values.shape[1]
    node_rows = cotangent.shape[0]
    width_in = features.shape[1]
    hid = cotangent.shape[1]
    row_blocks = COLS * node_rows // block_size
    col_blocks = ROWS * node_rows // block_size
    extra = hid + BIAS_ROWS
    shards = [swap(features, "row", k) for k in (1, 2)]
    outer = jnp.concatenate([features, swap(features, "row", 3)])
    tile = densify(block_values, block_rows, block_cols, block_count, row_blocks, col_blocks)
    cot_far = swap(cotangent, "col", 2)
    send = forward(False, tile, outer, shards)
    keep = forward(True, tile, outer, shards)
    sib, cot_far = lax.optimization_barrier((swap(send, "col", 1), cot_far))
    near = (keep + sib.astype(F32)).astype(BF16)
    far = swap(near, "col", 2)
    pre_act, grads = pl.pallas_call(
        layer_kernel,
        in_specs=[WHOLE] * 6,
        out_specs=[WHOLE] * 2,
        out_shape=[
            pltpu.VMEM((node_rows, hid), F32),
            jax.ShapeDtypeStruct((2 * node_rows + extra, width_in), BF16),
        ],
        compiler_params=LIMIT,
        name="layer",
    )(near, far, cotangent, cot_far, weight, bias.reshape(1, hid))
    block = jax.ShapeDtypeStruct((node_rows, width_in), BF16)
    part = pl.pallas_call(
        backward_mine_kernel,
        in_specs=[WHOLE] * 2,
        out_specs=WHOLE,
        out_shape=jax.ShapeDtypeStruct((ROWS, node_rows, width_in), F32),
        compiler_params=LIMIT,
        cost_estimate=pl.CostEstimate(flops=tile.size * width_in, bytes_accessed=tile.size, transcendentals=0),
        name="backward_mine",
    )(tile, grads)
    part, grads_sib = lax.optimization_barrier((part, swap(grads, "col", 1)))
    stripe = pl.pallas_call(
        stripe_kernel,
        in_specs=[WHOLE] * 2,
        out_specs=WHOLE,
        out_shape=jax.ShapeDtypeStruct((width_in + BIAS_ROWS, width_in), BF16),
        compiler_params=LIMIT,
        name="stripe",
    )(grads, grads_sib)
    stripe_far = swap(stripe, "row", 2)
    own, *sends = pl.pallas_call(
        backward_kernel,
        in_specs=[WHOLE] * 4,
        out_specs=[WHOLE] * 4,
        out_shape=[jax.ShapeDtypeStruct(block.shape, F32)] + [block] * 3,
        compiler_params=LIMIT,
        name="backward",
    )(tile, grads, grads_sib, part)
    pair = (stripe.astype(F32) + stripe_far.astype(F32)).astype(BF16)
    pair, sends[2] = lax.optimization_barrier((pair, sends[2]))
    got = [swap(send, "row", k) for k, send in zip((1, 2, 3), sends)]
    pair, pre_act = lax.optimization_barrier((pair, pre_act))
    hidden = (pre_act * jax.nn.sigmoid(pre_act)).astype(BF16)
    pair_far = swap(pair, "row", 1)
    gw_half = pair[:width_in].astype(F32) + pair_far[:width_in].astype(F32)
    gw_half, hidden = lax.optimization_barrier((gw_half, hidden))
    gw_sib = swap(gw_half, "col", 1)
    norm_scale = float(node_rows * ROWS * COLS) ** (-0.5)
    grad_features, hidden, grad_weight, grad_bias = pl.pallas_call(
        functools.partial(last_kernel, norm_scale),
        in_specs=[WHOLE] * 9,
        out_specs=[WHOLE] * 4,
        out_shape=[
            block,
            jax.ShapeDtypeStruct(hidden.shape, BF16),
            jax.ShapeDtypeStruct((width_in, hid), F32),
            jax.ShapeDtypeStruct((1, hid), F32),
        ],
        compiler_params=LIMIT,
        name="last",
    )(own, *got, hidden, pair, pair_far, gw_half, gw_sib)
    return hidden, grad_weight, grad_bias.reshape(hid), grad_features


def solution(mesh):
    in_specs = (
        P(("parts", "col", "row"), None),
        P(("parts", "row", "col"), None, None),
        P(("parts", "row", "col")),
        P(("parts", "row", "col")),
        P(("parts", "row", "col")),
        P(),
        P(),
        P(("parts", "row", "col"), None),
    )
    out_specs = (
        P(("parts", "row", "col"), None),
        P("parts", None),
        P("parts"),
        P(("parts", "col", "row"), None),
    )
    small = mesh.shape["row"] == ROWS and mesh.shape["col"] == COLS
    return jax.shard_map(
        dense_tile if small else by_slots,
        mesh=mesh,
        in_specs=in_specs,
        out_specs=out_specs,
        check_vma=False,
    )
```

```python
import functools

import jax
import jax.numpy as jnp
from jax import lax
from jax.experimental import pallas as pl
from jax.experimental.pallas import tpu as pltpu
from jax.sharding import PartitionSpec as P

F32 = jnp.float32
BF16 = jnp.bfloat16
ROWS = 4
COLS = 4
WHOLE = pl.BlockSpec(memory_space=pltpu.VMEM)
SCALARS = pl.BlockSpec(memory_space=pltpu.SMEM)
LIMIT = pltpu.CompilerParams(vmem_limit_bytes=16 * 2**20)
BIAS_ROWS = 16
GROUP = 8


def pick_rows(pick_index, live_mask, source_rows):
    source_count = source_rows.shape[0]
    onehot = (
        (pick_index[:, None] == jnp.arange(source_count, dtype=jnp.int32)[None, :])
        & live_mask[:, None]
    ).astype(jnp.bfloat16)
    chosen = jnp.dot(
        onehot, source_rows.reshape(source_count, -1), preferred_element_type=jnp.float32
    ).astype(jnp.bfloat16)
    return chosen.reshape((pick_index.shape[0],) + source_rows.shape[1:])


def slot_terms(values, pick_index, live_mask, source_rows, forward_pass):
    chosen = pick_rows(pick_index, live_mask, source_rows)
    if forward_pass:
        return jnp.einsum("spq,sqf->spf", values, chosen, preferred_element_type=jnp.float32)
    return jnp.einsum("spq,spf->sqf", values, chosen, preferred_element_type=jnp.float32)


def place_terms(products, place_index, blocks):
    block_ids = jnp.arange(blocks, dtype=jnp.int32)
    onehot = (block_ids[:, None] == place_index[None, :]).astype(jnp.bfloat16)
    flat = products.reshape(products.shape[0], -1)
    upper = flat.astype(jnp.bfloat16)
    lower = (flat - upper.astype(jnp.float32)).astype(jnp.bfloat16)
    placed = jnp.dot(onehot, upper, preferred_element_type=jnp.float32)
    placed = placed + jnp.dot(onehot, lower, preferred_element_type=jnp.float32)
    return placed.reshape(blocks * products.shape[1], products.shape[2])


def by_slots(features, block_values, block_rows, block_cols, block_count, weight, bias, cotangent):
    block_size = block_values.shape[1]
    slot_total = block_values.shape[0]
    live_mask = jnp.arange(slot_total, dtype=jnp.int32) < block_count[0]
    node_rows = cotangent.shape[0]
    width_in = features.shape[1]
    column_rows = lax.all_gather(features, "row", axis=0, tiled=True)
    column_blocks = column_rows.reshape(-1, block_size, width_in)
    forward_terms = slot_terms(block_values, block_cols, live_mask, column_blocks, True)
    aggregate = lax.psum_scatter(
        place_terms(
            forward_terms, block_rows, lax.axis_size("col") * node_rows // block_size
        ).astype(jnp.bfloat16),
        "col",
        scatter_dimension=0,
        tiled=True,
    ).astype(jnp.float32)
    aggregate = aggregate.astype(jnp.bfloat16)
    pre_act = jnp.dot(aggregate, weight, preferred_element_type=jnp.float32) + bias
    sigmoid_pre = jax.nn.sigmoid(pre_act)
    hidden = (pre_act * sigmoid_pre).astype(jnp.bfloat16)
    pre_grad = (
        cotangent.astype(jnp.float32) * sigmoid_pre * (1.0 + pre_act * (1.0 - sigmoid_pre))
    ).astype(jnp.bfloat16)
    grad_local = lax.dot_general(
        aggregate, pre_grad, (((0,), (0,)), ((), ())), preferred_element_type=jnp.float32
    )
    bias_local = jnp.sum(pre_grad.astype(jnp.float32), axis=0)
    grad_weight, grad_bias = lax.psum((grad_local, bias_local), ("row", "col"))
    norm_scale = float(node_rows * lax.axis_size("row") * lax.axis_size("col")) ** (-0.5)
    agg_grad = lax.dot_general(
        pre_grad, weight, (((1,), (1,)), ((), ())), preferred_element_type=jnp.float32
    ).astype(jnp.bfloat16)
    stripe_rows = lax.all_gather(agg_grad, "col", axis=0, tiled=True)
    stripe_blocks = stripe_rows.reshape(-1, block_size, width_in)
    backward_terms = slot_terms(block_values, block_rows, live_mask, stripe_blocks, False)
    grad_features = lax.psum_scatter(
        place_terms(
            backward_terms, block_cols, lax.axis_size("row") * node_rows // block_size
        ).astype(jnp.bfloat16),
        "row",
        scatter_dimension=0,
        tiled=True,
    )
    return (hidden, grad_weight * norm_scale, grad_bias * norm_scale, grad_features)


def densify_kernel(chunks, row_blocks, col_blocks, count_in, rows_in, cols_in, values_ref, tile_ref,
                   held, acc, count_ref, rows_ref, cols_ref, sems, scalar_sems):
    slots, block, _ = values_ref.shape
    size = slots // chunks
    scalars = [
        pltpu.make_async_copy(source, held_in, scalar_sems.at[i])
        for i, (source, held_in) in enumerate(
            ((count_in, count_ref), (rows_in, rows_ref), (cols_in, cols_ref))
        )
    ]
    copies = [
        pltpu.make_async_copy(
            values_ref.at[pl.ds(i * size, size)], held.at[pl.ds(i * size, size)], sems.at[i]
        )
        for i in range(chunks)
    ]
    for copy in scalars + copies:
        copy.start()
    acc[...] = jnp.zeros_like(acc)
    for copy in scalars:
        copy.wait()
    live = count_ref[0, 0]

    def add_slot(i, carry):
        place = rows_ref[i] * col_blocks + cols_ref[i]
        acc[place] = acc[place] + held[i].astype(F32)
        return carry

    def add_group(first, i, carry):
        for j in range(GROUP):
            add_slot(first + i * GROUP + j, carry)
        return carry

    for i, copy in enumerate(copies):
        copy.wait()
        here = jnp.clip(live - i * size, 0, size)
        groups = here // GROUP
        lax.fori_loop(0, groups, functools.partial(add_group, i * size), 0)
        lax.fori_loop(i * size + groups * GROUP, i * size + here, add_slot, 0)
    for r in range(row_blocks):
        for c in range(col_blocks):
            tile_ref[pl.ds(r * block, block), pl.ds(c * block, block)] = acc[
                r * col_blocks + c
            ].astype(BF16)


def densify(values, rows, cols, count, row_blocks, col_blocks):
    slots, block, _ = values.shape
    chunks = 8
    in_hbm = [
        pltpu.with_memory_space_constraint(array, pltpu.HBM)
        for array in (rows, cols, values)
    ]
    return pl.pallas_call(
        functools.partial(densify_kernel, chunks, row_blocks, col_blocks),
        in_specs=[WHOLE] + [pl.BlockSpec(memory_space=pltpu.HBM)] * 3,
        out_specs=WHOLE,
        out_shape=jax.ShapeDtypeStruct((row_blocks * block, col_blocks * block), BF16),
        scratch_shapes=[
            pltpu.VMEM(values.shape, BF16),
            pltpu.VMEM((row_blocks * col_blocks, block, block), F32),
            pltpu.SMEM((1, 1), jnp.int32),
            pltpu.SMEM(rows.shape, jnp.int32),
            pltpu.SMEM(cols.shape, jnp.int32),
            pltpu.SemaphoreType.DMA((chunks,)),
            pltpu.SemaphoreType.DMA((3,)),
        ],
        compiler_params=LIMIT,
        cost_estimate=pl.CostEstimate(flops=slots * block * block, bytes_accessed=values.size * 2, transcendentals=0),
        name="densify",
    )(count.reshape(1, 1), *in_hbm)


def forward_kernel(mine, tile_ref, outer_ref, x1, x2, out_ref):
    row = lax.axis_index("row")
    core = lax.rem(lax.axis_index("col"), 2)
    half = core if mine else 1 - core
    rows = x1.shape[0]
    for x in range(2):
        row_at = pl.multiple_of((2 * x + half) * rows, rows)
        total = None
        for k, shard in ((0, outer_ref[:rows, :]), (3, outer_ref[rows:, :]), (1, x1[...]), (2, x2[...])):
            col_at = pl.multiple_of(jnp.bitwise_xor(row, k) * rows, rows)
            tile = tile_ref[pl.ds(row_at, rows), pl.ds(col_at, rows)]
            term = jnp.dot(tile, shard, preferred_element_type=F32)
            total = term if total is None else total + term
        out_ref[pl.ds(x * rows, rows), :] = total.astype(out_ref.dtype)


def forward(mine, tile, outer, shards):
    rows, width_in = shards[0].shape
    return pl.pallas_call(
        functools.partial(forward_kernel, mine),
        in_specs=[WHOLE] * 4,
        out_specs=WHOLE,
        out_shape=jax.ShapeDtypeStruct((2 * rows, width_in), F32 if mine else BF16),
        compiler_params=LIMIT,
        cost_estimate=pl.CostEstimate(flops=tile.size * width_in, bytes_accessed=tile.size, transcendentals=0),
        name="forward_mine" if mine else "forward_sibling",
    )(tile, outer, *shards)


def layer_kernel(near_ref, far_ref, cot_ref, cot_far_ref, weight_ref, bias_ref, act_ref, swap_ref):
    mine = lax.rem(lax.axis_index("col") // 2, 2)
    rows, hid = cot_ref.shape
    width_in = near_ref.shape[1]
    weight = weight_ref[...]
    gw = None
    gb = None
    for other, source_ref in enumerate((cot_ref, cot_far_ref)):
        block = pl.ds(pl.multiple_of(jnp.bitwise_xor(mine, other) * rows, rows), rows)
        aggregate = (near_ref[block, :].astype(F32) + far_ref[block, :].astype(F32)).astype(BF16)
        pre_act = jnp.dot(aggregate, weight, preferred_element_type=F32) + bias_ref[...]
        sigmoid_pre = jax.nn.sigmoid(pre_act)
        if other == 0:
            act_ref[...] = pre_act
        cot = source_ref[...].astype(F32)
        pre_grad = (cot * sigmoid_pre * (1.0 + pre_act * (1.0 - sigmoid_pre))).astype(BF16)
        swap_ref[block, :] = lax.dot_general(
            pre_grad, weight, (((1,), (1,)), ((), ())), preferred_element_type=F32
        ).astype(BF16)
        term = lax.dot_general(
            aggregate, pre_grad, (((0,), (0,)), ((), ())), preferred_element_type=F32
        )
        bias_term = jnp.sum(pre_grad.astype(F32), axis=0, keepdims=True)
        gw = term if gw is None else gw + term
        gb = bias_term if gb is None else gb + bias_term
    at = 2 * rows
    for j in range(hid // width_in):
        lanes = slice(j * width_in, (j + 1) * width_in)
        swap_ref[pl.ds(at + j * width_in, width_in), :] = gw[:, lanes].astype(BF16)
    at = at + hid
    swap_ref[pl.ds(at, BIAS_ROWS), :] = jnp.concatenate(
        [gb[:, j * width_in : (j + 1) * width_in] for j in range(hid // width_in)]
        + [jnp.zeros((BIAS_ROWS - hid // width_in, width_in), F32)],
        axis=0,
    ).astype(BF16)


def backward_terms(tile_ref, half, k, grad_ref, rows):
    col_at = pl.multiple_of(jnp.bitwise_xor(lax.axis_index("row"), k) * rows, rows)
    total = None
    for x in range(2):
        row_at = pl.multiple_of((2 * x + half) * rows, rows)
        term = lax.dot_general(
            tile_ref[pl.ds(row_at, rows), pl.ds(col_at, rows)],
            grad_ref[pl.ds(x * rows, rows), :],
            (((0,), (0,)), ((), ())),
            preferred_element_type=F32,
        )
        total = term if total is None else total + term
    return total


def backward_mine_kernel(tile_ref, own_ref, part_ref):
    core = lax.rem(lax.axis_index("col"), 2)
    for k in range(ROWS):
        part_ref[k] = backward_terms(tile_ref, core, k, own_ref, part_ref.shape[1])


def turn_kernel(tile_ref, turned_ref):
    core = lax.rem(lax.axis_index("col"), 2)
    width = turned_ref.shape[1] // 2
    for x in range(2):
        row_at = pl.multiple_of((2 * x + 1 - core) * width, width)
        for c in range(turned_ref.shape[0] // width):
            lanes = slice(c * width, (c + 1) * width)
            turned_ref[lanes, x * width : (x + 1) * width] = tile_ref[pl.ds(row_at, width), lanes].T


def backward_kernel(offsets, turned_ref, sib_ref, part_ref, *outs):
    row = lax.axis_index("row")
    rows = part_ref.shape[1]
    for k, out in zip(offsets, outs):
        at = pl.multiple_of(jnp.bitwise_xor(row, k) * rows, rows)
        total = part_ref[k] + jnp.dot(
            turned_ref[pl.ds(at, rows), :], sib_ref[pl.ds(0, 2 * rows), :], preferred_element_type=F32
        )
        out[...] = total.astype(out.dtype)


def backward(offsets, turned, sib, part):
    _, rows, width_in = part.shape
    return pl.pallas_call(
        functools.partial(backward_kernel, offsets),
        in_specs=[WHOLE] * 3,
        out_specs=[WHOLE] * len(offsets),
        out_shape=[jax.ShapeDtypeStruct((rows, width_in), BF16 if k else F32) for k in offsets],
        compiler_params=LIMIT,
        name="backward",
    )(turned, sib, part)


def stripe_kernel(own_ref, sib_ref, stripe_ref):
    core = lax.rem(lax.axis_index("col"), 2)
    width_in = own_ref.shape[1]
    first = own_ref.shape[0] - BIAS_ROWS - 2 * width_in
    for source, target, size in (
        (pl.multiple_of(first + core * width_in, BIAS_ROWS), 0, width_in),
        (own_ref.shape[0] - BIAS_ROWS, width_in, BIAS_ROWS),
    ):
        stripe_ref[pl.ds(target, size), :] = (
            own_ref[pl.ds(source, size), :].astype(F32) + sib_ref[pl.ds(source, size), :].astype(F32)
        ).astype(BF16)


def last_kernel(scale, keep_ref, got1, got2, got3, act_ref, pair_ref, pair_far_ref, half_ref, sib_ref,
                features_ref, hidden_ref, gw_ref, gb_ref):
    core = lax.rem(lax.axis_index("col"), 2)
    width_in, hid = gw_ref.shape
    half = half_ref[...] * scale
    sib = sib_ref[...] * scale
    for j in range(2):
        gw_ref[:, j * width_in : (j + 1) * width_in] = jnp.where(core == j, half, sib)
    block = pl.ds(width_in, BIAS_ROWS)
    both = (pair_ref[block, :].astype(F32) + pair_far_ref[block, :].astype(F32)) * scale
    for j in range(hid // width_in):
        gb_ref[:, j * width_in : (j + 1) * width_in] = both[j : j + 1, :]
    total = keep_ref[...] + got1[...].astype(F32)
    total = total + got2[...].astype(F32) + got3[...].astype(F32)
    features_ref[...] = total.astype(BF16)
    hidden_ref[...] = act_ref[...]


def swap(array, axis, bit):
    size = lax.axis_size(axis)
    return lax.ppermute(array, axis, [(i, i ^ bit) for i in range(size)])


def dense_tile(features, block_values, block_rows, block_cols, block_count, weight, bias, cotangent):
    block_size = block_values.shape[1]
    node_rows = cotangent.shape[0]
    width_in = features.shape[1]
    hid = cotangent.shape[1]
    row_blocks = COLS * node_rows // block_size
    col_blocks = ROWS * node_rows // block_size
    extra = hid + BIAS_ROWS
    shards = [swap(features, "row", k) for k in (1, 2)]
    outer = jnp.concatenate([features, swap(features, "row", 3)])
    tile = densify(block_values, block_rows, block_cols, block_count, row_blocks, col_blocks)
    cot_far = swap(cotangent, "col", 2)
    send = forward(False, tile, outer, shards)
    keep = forward(True, tile, outer, shards)
    sib, cot_far = lax.optimization_barrier((swap(send, "col", 1), cot_far))
    near = (keep + sib.astype(F32)).astype(BF16)
    near, tile = lax.optimization_barrier((near, tile))
    turned = pl.pallas_call(
        turn_kernel,
        in_specs=[WHOLE],
        out_specs=WHOLE,
        out_shape=jax.ShapeDtypeStruct((ROWS * node_rows, 2 * node_rows), BF16),
        compiler_params=LIMIT,
        name="turn",
    )(tile)
    far, turned = lax.optimization_barrier((swap(near, "col", 2), turned))
    pre_act, grads = pl.pallas_call(
        layer_kernel,
        in_specs=[WHOLE] * 6,
        out_specs=[WHOLE] * 2,
        out_shape=[
            pltpu.VMEM((node_rows, hid), F32),
            jax.ShapeDtypeStruct((2 * node_rows + extra, width_in), BF16),
        ],
        compiler_params=LIMIT,
        name="layer",
    )(near, far, cotangent, cot_far, weight, bias.reshape(1, hid))
    block = jax.ShapeDtypeStruct((node_rows, width_in), BF16)
    part = pl.pallas_call(
        backward_mine_kernel,
        in_specs=[WHOLE] * 2,
        out_specs=WHOLE,
        out_shape=jax.ShapeDtypeStruct((ROWS, node_rows, width_in), F32),
        compiler_params=LIMIT,
        cost_estimate=pl.CostEstimate(flops=tile.size * width_in, bytes_accessed=tile.size, transcendentals=0),
        name="backward_mine",
    )(tile, grads)
    part, grads_sib = lax.optimization_barrier((part, swap(grads, "col", 1)))
    stripe = pl.pallas_call(
        stripe_kernel,
        in_specs=[WHOLE] * 2,
        out_specs=WHOLE,
        out_shape=jax.ShapeDtypeStruct((width_in + BIAS_ROWS, width_in), BF16),
        compiler_params=LIMIT,
        name="stripe",
    )(grads, grads_sib)
    stripe_far = swap(stripe, "row", 2)
    first, second = backward((1, 2), turned, grads_sib, part)
    third, own = backward((3, 0), turned, grads_sib, part)
    stripe_far, third = lax.optimization_barrier((stripe_far, third))
    sends = [first, second, third]
    pair = (stripe.astype(F32) + stripe_far.astype(F32)).astype(BF16)
    pair, sends[2] = lax.optimization_barrier((pair, sends[2]))
    got = [swap(send, "row", k) for k, send in zip((1, 2, 3), sends)]
    pair, pre_act = lax.optimization_barrier((pair, pre_act))
    hidden = (pre_act * jax.nn.sigmoid(pre_act)).astype(BF16)
    pair_far = swap(pair, "row", 1)
    gw_half = pair[:width_in].astype(F32) + pair_far[:width_in].astype(F32)
    gw_half, hidden = lax.optimization_barrier((gw_half, hidden))
    gw_sib = swap(gw_half, "col", 1)
    norm_scale = float(node_rows * ROWS * COLS) ** (-0.5)
    grad_features, hidden, grad_weight, grad_bias = pl.pallas_call(
        functools.partial(last_kernel, norm_scale),
        in_specs=[WHOLE] * 9,
        out_specs=[WHOLE] * 4,
        out_shape=[
            block,
            jax.ShapeDtypeStruct(hidden.shape, BF16),
            jax.ShapeDtypeStruct((width_in, hid), F32),
            jax.ShapeDtypeStruct((1, hid), F32),
        ],
        compiler_params=LIMIT,
        name="last",
    )(own, *got, hidden, pair, pair_far, gw_half, gw_sib)
    return hidden, grad_weight, grad_bias.reshape(hid), grad_features


def solution(mesh):
    in_specs = (
        P(("parts", "col", "row"), None),
        P(("parts", "row", "col"), None, None),
        P(("parts", "row", "col")),
        P(("parts", "row", "col")),
        P(("parts", "row", "col")),
        P(),
        P(),
        P(("parts", "row", "col"), None),
    )
    out_specs = (
        P(("parts", "row", "col"), None),
        P("parts", None),
        P("parts"),
        P(("parts", "col", "row"), None),
    )
    small = mesh.shape["row"] == ROWS and mesh.shape["col"] == COLS
    return jax.shard_map(
        dense_tile if small else by_slots,
        mesh=mesh,
        in_specs=in_specs,
        out_specs=out_specs,
        check_vma=False,
    )
```

```python
import functools

import jax
import jax.numpy as jnp
from jax import lax
from jax.experimental import pallas as pl
from jax.experimental.pallas import tpu as pltpu
from jax.sharding import PartitionSpec as P

F32 = jnp.float32
BF16 = jnp.bfloat16
ROWS = 4
COLS = 4
WHOLE = pl.BlockSpec(memory_space=pltpu.VMEM)
SCALARS = pl.BlockSpec(memory_space=pltpu.SMEM)
LIMIT = pltpu.CompilerParams(vmem_limit_bytes=16 * 2**20)
BIAS_ROWS = 16
GROUP = 8


def pick_rows(pick_index, live_mask, source_rows):
    source_count = source_rows.shape[0]
    onehot = (
        (pick_index[:, None] == jnp.arange(source_count, dtype=jnp.int32)[None, :])
        & live_mask[:, None]
    ).astype(jnp.bfloat16)
    chosen = jnp.dot(
        onehot, source_rows.reshape(source_count, -1), preferred_element_type=jnp.float32
    ).astype(jnp.bfloat16)
    return chosen.reshape((pick_index.shape[0],) + source_rows.shape[1:])


def slot_terms(values, pick_index, live_mask, source_rows, forward_pass):
    chosen = pick_rows(pick_index, live_mask, source_rows)
    if forward_pass:
        return jnp.einsum("spq,sqf->spf", values, chosen, preferred_element_type=jnp.float32)
    return jnp.einsum("spq,spf->sqf", values, chosen, preferred_element_type=jnp.float32)


def place_terms(products, place_index, blocks):
    block_ids = jnp.arange(blocks, dtype=jnp.int32)
    onehot = (block_ids[:, None] == place_index[None, :]).astype(jnp.bfloat16)
    flat = products.reshape(products.shape[0], -1)
    upper = flat.astype(jnp.bfloat16)
    lower = (flat - upper.astype(jnp.float32)).astype(jnp.bfloat16)
    placed = jnp.dot(onehot, upper, preferred_element_type=jnp.float32)
    placed = placed + jnp.dot(onehot, lower, preferred_element_type=jnp.float32)
    return placed.reshape(blocks * products.shape[1], products.shape[2])


def by_slots(features, block_values, block_rows, block_cols, block_count, weight, bias, cotangent):
    block_size = block_values.shape[1]
    slot_total = block_values.shape[0]
    live_mask = jnp.arange(slot_total, dtype=jnp.int32) < block_count[0]
    node_rows = cotangent.shape[0]
    width_in = features.shape[1]
    column_rows = lax.all_gather(features, "row", axis=0, tiled=True)
    column_blocks = column_rows.reshape(-1, block_size, width_in)
    forward_terms = slot_terms(block_values, block_cols, live_mask, column_blocks, True)
    aggregate = lax.psum_scatter(
        place_terms(
            forward_terms, block_rows, lax.axis_size("col") * node_rows // block_size
        ).astype(jnp.bfloat16),
        "col",
        scatter_dimension=0,
        tiled=True,
    ).astype(jnp.float32)
    aggregate = aggregate.astype(jnp.bfloat16)
    pre_act = jnp.dot(aggregate, weight, preferred_element_type=jnp.float32) + bias
    sigmoid_pre = jax.nn.sigmoid(pre_act)
    hidden = (pre_act * sigmoid_pre).astype(jnp.bfloat16)
    pre_grad = (
        cotangent.astype(jnp.float32) * sigmoid_pre * (1.0 + pre_act * (1.0 - sigmoid_pre))
    ).astype(jnp.bfloat16)
    grad_local = lax.dot_general(
        aggregate, pre_grad, (((0,), (0,)), ((), ())), preferred_element_type=jnp.float32
    )
    bias_local = jnp.sum(pre_grad.astype(jnp.float32), axis=0)
    grad_weight, grad_bias = lax.psum((grad_local, bias_local), ("row", "col"))
    norm_scale = float(node_rows * lax.axis_size("row") * lax.axis_size("col")) ** (-0.5)
    agg_grad = lax.dot_general(
        pre_grad, weight, (((1,), (1,)), ((), ())), preferred_element_type=jnp.float32
    ).astype(jnp.bfloat16)
    stripe_rows = lax.all_gather(agg_grad, "col", axis=0, tiled=True)
    stripe_blocks = stripe_rows.reshape(-1, block_size, width_in)
    backward_terms = slot_terms(block_values, block_rows, live_mask, stripe_blocks, False)
    grad_features = lax.psum_scatter(
        place_terms(
            backward_terms, block_cols, lax.axis_size("row") * node_rows // block_size
        ).astype(jnp.bfloat16),
        "row",
        scatter_dimension=0,
        tiled=True,
    )
    return (hidden, grad_weight * norm_scale, grad_bias * norm_scale, grad_features)


def densify_kernel(chunks, row_blocks, col_blocks, count_in, rows_in, cols_in, values_ref, tile_ref,
                   held, acc, count_ref, rows_ref, cols_ref, sems, scalar_sems):
    slots, block, _ = values_ref.shape
    size = slots // chunks
    scalars = [
        pltpu.make_async_copy(source, held_in, scalar_sems.at[i])
        for i, (source, held_in) in enumerate(
            ((count_in, count_ref), (rows_in, rows_ref), (cols_in, cols_ref))
        )
    ]
    copies = [
        pltpu.make_async_copy(
            values_ref.at[pl.ds(i * size, size)], held.at[pl.ds(i * size, size)], sems.at[i]
        )
        for i in range(chunks)
    ]
    for copy in scalars + copies:
        copy.start()
    acc[...] = jnp.zeros_like(acc)
    for copy in scalars:
        copy.wait()
    live = count_ref[0, 0]

    def add_slot(i, carry):
        place = rows_ref[i] * col_blocks + cols_ref[i]
        acc[place] = acc[place] + held[i].astype(F32)
        return carry

    def add_group(first, i, carry):
        for j in range(GROUP):
            add_slot(first + i * GROUP + j, carry)
        return carry

    for i, copy in enumerate(copies):
        copy.wait()
        here = jnp.clip(live - i * size, 0, size)
        groups = here // GROUP
        lax.fori_loop(0, groups, functools.partial(add_group, i * size), 0)
        lax.fori_loop(i * size + groups * GROUP, i * size + here, add_slot, 0)
    for r in range(row_blocks):
        for c in range(col_blocks):
            tile_ref[pl.ds(r * block, block), pl.ds(c * block, block)] = acc[
                r * col_blocks + c
            ].astype(BF16)


def densify(values, rows, cols, count, row_blocks, col_blocks):
    slots, block, _ = values.shape
    chunks = 8
    in_hbm = [
        pltpu.with_memory_space_constraint(array, pltpu.HBM)
        for array in (rows, cols, values)
    ]
    return pl.pallas_call(
        functools.partial(densify_kernel, chunks, row_blocks, col_blocks),
        in_specs=[WHOLE] + [pl.BlockSpec(memory_space=pltpu.HBM)] * 3,
        out_specs=WHOLE,
        out_shape=jax.ShapeDtypeStruct((row_blocks * block, col_blocks * block), BF16),
        scratch_shapes=[
            pltpu.VMEM(values.shape, BF16),
            pltpu.VMEM((row_blocks * col_blocks, block, block), F32),
            pltpu.SMEM((1, 1), jnp.int32),
            pltpu.SMEM(rows.shape, jnp.int32),
            pltpu.SMEM(cols.shape, jnp.int32),
            pltpu.SemaphoreType.DMA((chunks,)),
            pltpu.SemaphoreType.DMA((3,)),
        ],
        compiler_params=LIMIT,
        cost_estimate=pl.CostEstimate(flops=slots * block * block, bytes_accessed=values.size * 2, transcendentals=0),
        name="densify",
    )(count.reshape(1, 1), *in_hbm)


def forward_kernel(mine, tile_ref, outer_ref, x1, x2, out_ref):
    row = lax.axis_index("row")
    core = lax.rem(lax.axis_index("col"), 2)
    half = core if mine else 1 - core
    rows = x1.shape[0]
    for x in range(2):
        row_at = pl.multiple_of((2 * x + half) * rows, rows)
        total = None
        for k, shard in ((0, outer_ref[:rows, :]), (3, outer_ref[rows:, :]), (1, x1[...]), (2, x2[...])):
            col_at = pl.multiple_of(jnp.bitwise_xor(row, k) * rows, rows)
            tile = tile_ref[pl.ds(row_at, rows), pl.ds(col_at, rows)]
            term = jnp.dot(tile, shard, preferred_element_type=F32)
            total = term if total is None else total + term
        out_ref[pl.ds(x * rows, rows), :] = total.astype(out_ref.dtype)


def forward(mine, tile, outer, shards):
    rows, width_in = shards[0].shape
    return pl.pallas_call(
        functools.partial(forward_kernel, mine),
        in_specs=[WHOLE] * 4,
        out_specs=WHOLE,
        out_shape=jax.ShapeDtypeStruct((2 * rows, width_in), F32 if mine else BF16),
        compiler_params=LIMIT,
        cost_estimate=pl.CostEstimate(flops=tile.size * width_in, bytes_accessed=tile.size, transcendentals=0),
        name="forward_mine" if mine else "forward_sibling",
    )(tile, outer, *shards)


def layer_kernel(near_ref, far_ref, cot_ref, cot_far_ref, weight_ref, bias_ref, act_ref, swap_ref):
    mine = lax.rem(lax.axis_index("col") // 2, 2)
    rows, hid = cot_ref.shape
    width_in = near_ref.shape[1]
    weight = weight_ref[...]
    gw = None
    gb = None
    for other, source_ref in enumerate((cot_ref, cot_far_ref)):
        block = pl.ds(pl.multiple_of(jnp.bitwise_xor(mine, other) * rows, rows), rows)
        aggregate = (near_ref[block, :].astype(F32) + far_ref[block, :].astype(F32)).astype(BF16)
        pre_act = jnp.dot(aggregate, weight, preferred_element_type=F32) + bias_ref[...]
        sigmoid_pre = jax.nn.sigmoid(pre_act)
        if other == 0:
            act_ref[...] = pre_act
        cot = source_ref[...].astype(F32)
        pre_grad = (cot * sigmoid_pre * (1.0 + pre_act * (1.0 - sigmoid_pre))).astype(BF16)
        swap_ref[block, :] = lax.dot_general(
            pre_grad, weight, (((1,), (1,)), ((), ())), preferred_element_type=F32
        ).astype(BF16)
        term = lax.dot_general(
            aggregate, pre_grad, (((0,), (0,)), ((), ())), preferred_element_type=F32
        )
        bias_term = jnp.sum(pre_grad.astype(F32), axis=0, keepdims=True)
        gw = term if gw is None else gw + term
        gb = bias_term if gb is None else gb + bias_term
    at = 2 * rows
    for j in range(hid // width_in):
        lanes = slice(j * width_in, (j + 1) * width_in)
        swap_ref[pl.ds(at + j * width_in, width_in), :] = gw[:, lanes].astype(BF16)
    at = at + hid
    swap_ref[pl.ds(at, BIAS_ROWS), :] = jnp.concatenate(
        [gb[:, j * width_in : (j + 1) * width_in] for j in range(hid // width_in)]
        + [jnp.zeros((BIAS_ROWS - hid // width_in, width_in), F32)],
        axis=0,
    ).astype(BF16)


def backward_terms(tile_ref, half, k, grad_ref, rows):
    col_at = pl.multiple_of(jnp.bitwise_xor(lax.axis_index("row"), k) * rows, rows)
    total = None
    for x in range(2):
        row_at = pl.multiple_of((2 * x + half) * rows, rows)
        term = lax.dot_general(
            tile_ref[pl.ds(row_at, rows), pl.ds(col_at, rows)],
            grad_ref[pl.ds(x * rows, rows), :],
            (((0,), (0,)), ((), ())),
            preferred_element_type=F32,
        )
        total = term if total is None else total + term
    return total


def backward_mine_kernel(tile_ref, own_ref, part_ref):
    core = lax.rem(lax.axis_index("col"), 2)
    for k in range(ROWS):
        part_ref[k] = backward_terms(tile_ref, core, k, own_ref, part_ref.shape[1])


def turn_kernel(tile_ref, turned_ref):
    core = lax.rem(lax.axis_index("col"), 2)
    width = turned_ref.shape[1] // 2
    for x in range(2):
        row_at = pl.multiple_of((2 * x + 1 - core) * width, width)
        for c in range(turned_ref.shape[0] // width):
            lanes = slice(c * width, (c + 1) * width)
            turned_ref[lanes, x * width : (x + 1) * width] = tile_ref[pl.ds(row_at, width), lanes].T


def backward_kernel(turned_ref, sib_ref, part_ref, keep_ref, send1, send2, send3):
    row = lax.axis_index("row")
    rows = keep_ref.shape[0]
    for k, out in ((1, send1), (2, send2), (3, send3), (0, keep_ref)):
        at = pl.multiple_of(jnp.bitwise_xor(row, k) * rows, rows)
        total = part_ref[k] + jnp.dot(
            turned_ref[pl.ds(at, rows), :], sib_ref[pl.ds(0, 2 * rows), :], preferred_element_type=F32
        )
        out[...] = total.astype(out.dtype)


def stripe_kernel(own_ref, sib_ref, stripe_ref):
    core = lax.rem(lax.axis_index("col"), 2)
    width_in = own_ref.shape[1]
    first = own_ref.shape[0] - BIAS_ROWS - 2 * width_in
    for source, target, size in (
        (pl.multiple_of(first + core * width_in, BIAS_ROWS), 0, width_in),
        (own_ref.shape[0] - BIAS_ROWS, width_in, BIAS_ROWS),
    ):
        stripe_ref[pl.ds(target, size), :] = (
            own_ref[pl.ds(source, size), :].astype(F32) + sib_ref[pl.ds(source, size), :].astype(F32)
        ).astype(BF16)


def last_kernel(scale, keep_ref, got1, got2, got3, act_ref, pair_ref, pair_far_ref, half_ref, sib_ref,
                features_ref, hidden_ref, gw_ref, gb_ref):
    core = lax.rem(lax.axis_index("col"), 2)
    width_in, hid = gw_ref.shape
    half = half_ref[...] * scale
    sib = sib_ref[...] * scale
    for j in range(2):
        gw_ref[:, j * width_in : (j + 1) * width_in] = jnp.where(core == j, half, sib)
    block = pl.ds(width_in, BIAS_ROWS)
    both = (pair_ref[block, :].astype(F32) + pair_far_ref[block, :].astype(F32)) * scale
    for j in range(hid // width_in):
        gb_ref[:, j * width_in : (j + 1) * width_in] = both[j : j + 1, :]
    total = keep_ref[...] + got1[...].astype(F32)
    total = total + got2[...].astype(F32) + got3[...].astype(F32)
    features_ref[...] = total.astype(BF16)
    hidden_ref[...] = act_ref[...]


def swap(array, axis, bit):
    size = lax.axis_size(axis)
    return lax.ppermute(array, axis, [(i, i ^ bit) for i in range(size)])


def dense_tile(features, block_values, block_rows, block_cols, block_count, weight, bias, cotangent):
    block_size = block_values.shape[1]
    node_rows = cotangent.shape[0]
    width_in = features.shape[1]
    hid = cotangent.shape[1]
    row_blocks = COLS * node_rows // block_size
    col_blocks = ROWS * node_rows // block_size
    extra = hid + BIAS_ROWS
    shards = [swap(features, "row", k) for k in (1, 2)]
    outer = jnp.concatenate([features, swap(features, "row", 3)])
    tile = densify(block_values, block_rows, block_cols, block_count, row_blocks, col_blocks)
    cot_far = swap(cotangent, "col", 2)
    send = forward(False, tile, outer, shards)
    keep = forward(True, tile, outer, shards)
    sib, cot_far = lax.optimization_barrier((swap(send, "col", 1), cot_far))
    near = (keep + sib.astype(F32)).astype(BF16)
    near, tile = lax.optimization_barrier((near, tile))
    turned = pl.pallas_call(
        turn_kernel,
        in_specs=[WHOLE],
        out_specs=WHOLE,
        out_shape=jax.ShapeDtypeStruct((ROWS * node_rows, 2 * node_rows), BF16),
        compiler_params=LIMIT,
        name="turn",
    )(tile)
    far, turned = lax.optimization_barrier((swap(near, "col", 2), turned))
    pre_act, grads = pl.pallas_call(
        layer_kernel,
        in_specs=[WHOLE] * 6,
        out_specs=[WHOLE] * 2,
        out_shape=[
            pltpu.VMEM((node_rows, hid), F32),
            jax.ShapeDtypeStruct((2 * node_rows + extra, width_in), BF16),
        ],
        compiler_params=LIMIT,
        name="layer",
    )(near, far, cotangent, cot_far, weight, bias.reshape(1, hid))
    block = jax.ShapeDtypeStruct((node_rows, width_in), BF16)
    part = pl.pallas_call(
        backward_mine_kernel,
        in_specs=[WHOLE] * 2,
        out_specs=WHOLE,
        out_shape=jax.ShapeDtypeStruct((ROWS, node_rows, width_in), F32),
        compiler_params=LIMIT,
        cost_estimate=pl.CostEstimate(flops=tile.size * width_in, bytes_accessed=tile.size, transcendentals=0),
        name="backward_mine",
    )(tile, grads)
    part, grads_sib = lax.optimization_barrier((part, swap(grads, "col", 1)))
    stripe = pl.pallas_call(
        stripe_kernel,
        in_specs=[WHOLE] * 2,
        out_specs=WHOLE,
        out_shape=jax.ShapeDtypeStruct((width_in + BIAS_ROWS, width_in), BF16),
        compiler_params=LIMIT,
        name="stripe",
    )(grads, grads_sib)
    stripe_far = swap(stripe, "row", 2)
    own, *sends = pl.pallas_call(
        backward_kernel,
        in_specs=[WHOLE] * 3,
        out_specs=[WHOLE] * 4,
        out_shape=[jax.ShapeDtypeStruct(block.shape, F32)] + [block] * 3,
        compiler_params=LIMIT,
        name="backward",
    )(turned, grads_sib, part)
    pair = (stripe.astype(F32) + stripe_far.astype(F32)).astype(BF16)
    pair, sends[2] = lax.optimization_barrier((pair, sends[2]))
    got = [swap(send, "row", k) for k, send in zip((1, 2, 3), sends)]
    pair, pre_act = lax.optimization_barrier((pair, pre_act))
    hidden = (pre_act * jax.nn.sigmoid(pre_act)).astype(BF16)
    pair_far = swap(pair, "row", 1)
    gw_half = pair[:width_in].astype(F32) + pair_far[:width_in].astype(F32)
    gw_half, hidden = lax.optimization_barrier((gw_half, hidden))
    gw_sib = swap(gw_half, "col", 1)
    norm_scale = float(node_rows * ROWS * COLS) ** (-0.5)
    grad_features, hidden, grad_weight, grad_bias = pl.pallas_call(
        functools.partial(last_kernel, norm_scale),
        in_specs=[WHOLE] * 9,
        out_specs=[WHOLE] * 4,
        out_shape=[
            block,
            jax.ShapeDtypeStruct(hidden.shape, BF16),
            jax.ShapeDtypeStruct((width_in, hid), F32),
            jax.ShapeDtypeStruct((1, hid), F32),
        ],
        compiler_params=LIMIT,
        name="last",
    )(own, *got, hidden, pair, pair_far, gw_half, gw_sib)
    return hidden, grad_weight, grad_bias.reshape(hid), grad_features


def solution(mesh):
    in_specs = (
        P(("parts", "col", "row"), None),
        P(("parts", "row", "col"), None, None),
        P(("parts", "row", "col")),
        P(("parts", "row", "col")),
        P(("parts", "row", "col")),
        P(),
        P(),
        P(("parts", "row", "col"), None),
    )
    out_specs = (
        P(("parts", "row", "col"), None),
        P("parts", None),
        P("parts"),
        P(("parts", "col", "row"), None),
    )
    small = mesh.shape["row"] == ROWS and mesh.shape["col"] == COLS
    return jax.shard_map(
        dense_tile if small else by_slots,
        mesh=mesh,
        in_specs=in_specs,
        out_specs=out_specs,
        check_vma=False,
    )
```

```python
import functools

import jax
import jax.numpy as jnp
from jax import lax
from jax.experimental import pallas as pl
from jax.experimental.pallas import tpu as pltpu
from jax.sharding import PartitionSpec as P

F32 = jnp.float32
BF16 = jnp.bfloat16
ROWS = 4
COLS = 4
WHOLE = pl.BlockSpec(memory_space=pltpu.VMEM)
SCALARS = pl.BlockSpec(memory_space=pltpu.SMEM)
LIMIT = pltpu.CompilerParams(vmem_limit_bytes=16 * 2**20)
BIAS_ROWS = 16
GROUP = 8


def pick_rows(pick_index, live_mask, source_rows):
    source_count = source_rows.shape[0]
    onehot = (
        (pick_index[:, None] == jnp.arange(source_count, dtype=jnp.int32)[None, :])
        & live_mask[:, None]
    ).astype(jnp.bfloat16)
    chosen = jnp.dot(
        onehot, source_rows.reshape(source_count, -1), preferred_element_type=jnp.float32
    ).astype(jnp.bfloat16)
    return chosen.reshape((pick_index.shape[0],) + source_rows.shape[1:])


def slot_terms(values, pick_index, live_mask, source_rows, forward_pass):
    chosen = pick_rows(pick_index, live_mask, source_rows)
    if forward_pass:
        return jnp.einsum("spq,sqf->spf", values, chosen, preferred_element_type=jnp.float32)
    return jnp.einsum("spq,spf->sqf", values, chosen, preferred_element_type=jnp.float32)


def place_terms(products, place_index, blocks):
    block_ids = jnp.arange(blocks, dtype=jnp.int32)
    onehot = (block_ids[:, None] == place_index[None, :]).astype(jnp.bfloat16)
    flat = products.reshape(products.shape[0], -1)
    upper = flat.astype(jnp.bfloat16)
    lower = (flat - upper.astype(jnp.float32)).astype(jnp.bfloat16)
    placed = jnp.dot(onehot, upper, preferred_element_type=jnp.float32)
    placed = placed + jnp.dot(onehot, lower, preferred_element_type=jnp.float32)
    return placed.reshape(blocks * products.shape[1], products.shape[2])


def by_slots(features, block_values, block_rows, block_cols, block_count, weight, bias, cotangent):
    block_size = block_values.shape[1]
    slot_total = block_values.shape[0]
    live_mask = jnp.arange(slot_total, dtype=jnp.int32) < block_count[0]
    node_rows = cotangent.shape[0]
    width_in = features.shape[1]
    column_rows = lax.all_gather(features, "row", axis=0, tiled=True)
    column_blocks = column_rows.reshape(-1, block_size, width_in)
    forward_terms = slot_terms(block_values, block_cols, live_mask, column_blocks, True)
    aggregate = lax.psum_scatter(
        place_terms(
            forward_terms, block_rows, lax.axis_size("col") * node_rows // block_size
        ).astype(jnp.bfloat16),
        "col",
        scatter_dimension=0,
        tiled=True,
    ).astype(jnp.float32)
    aggregate = aggregate.astype(jnp.bfloat16)
    pre_act = jnp.dot(aggregate, weight, preferred_element_type=jnp.float32) + bias
    sigmoid_pre = jax.nn.sigmoid(pre_act)
    hidden = (pre_act * sigmoid_pre).astype(jnp.bfloat16)
    pre_grad = (
        cotangent.astype(jnp.float32) * sigmoid_pre * (1.0 + pre_act * (1.0 - sigmoid_pre))
    ).astype(jnp.bfloat16)
    grad_local = lax.dot_general(
        aggregate, pre_grad, (((0,), (0,)), ((), ())), preferred_element_type=jnp.float32
    )
    bias_local = jnp.sum(pre_grad.astype(jnp.float32), axis=0)
    grad_weight, grad_bias = lax.psum((grad_local, bias_local), ("row", "col"))
    norm_scale = float(node_rows * lax.axis_size("row") * lax.axis_size("col")) ** (-0.5)
    agg_grad = lax.dot_general(
        pre_grad, weight, (((1,), (1,)), ((), ())), preferred_element_type=jnp.float32
    ).astype(jnp.bfloat16)
    stripe_rows = lax.all_gather(agg_grad, "col", axis=0, tiled=True)
    stripe_blocks = stripe_rows.reshape(-1, block_size, width_in)
    backward_terms = slot_terms(block_values, block_rows, live_mask, stripe_blocks, False)
    grad_features = lax.psum_scatter(
        place_terms(
            backward_terms, block_cols, lax.axis_size("row") * node_rows // block_size
        ).astype(jnp.bfloat16),
        "row",
        scatter_dimension=0,
        tiled=True,
    )
    return (hidden, grad_weight * norm_scale, grad_bias * norm_scale, grad_features)


def densify_kernel(chunks, row_blocks, col_blocks, count_in, rows_in, cols_in, values_ref, tile_ref,
                   held, acc, count_ref, rows_ref, cols_ref, sems, scalar_sems):
    slots, block, _ = values_ref.shape
    size = slots // chunks
    scalars = [
        pltpu.make_async_copy(source, held_in, scalar_sems.at[i])
        for i, (source, held_in) in enumerate(
            ((count_in, count_ref), (rows_in, rows_ref), (cols_in, cols_ref))
        )
    ]
    copies = [
        pltpu.make_async_copy(
            values_ref.at[pl.ds(i * size, size)], held.at[pl.ds(i * size, size)], sems.at[i]
        )
        for i in range(chunks)
    ]
    for copy in scalars + copies:
        copy.start()
    acc[...] = jnp.zeros_like(acc)
    for copy in scalars:
        copy.wait()
    live = count_ref[0, 0]

    def add_slot(i, carry):
        place = rows_ref[i] * col_blocks + cols_ref[i]
        acc[place] = acc[place] + held[i].astype(F32)
        return carry

    def add_group(first, i, carry):
        for j in range(GROUP):
            add_slot(first + i * GROUP + j, carry)
        return carry

    for i, copy in enumerate(copies):
        copy.wait()
        here = jnp.clip(live - i * size, 0, size)
        groups = here // GROUP
        lax.fori_loop(0, groups, functools.partial(add_group, i * size), 0)
        lax.fori_loop(i * size + groups * GROUP, i * size + here, add_slot, 0)
    for r in range(row_blocks):
        for c in range(col_blocks):
            tile_ref[pl.ds(r * block, block), pl.ds(c * block, block)] = acc[
                r * col_blocks + c
            ].astype(BF16)


def densify(values, rows, cols, count, row_blocks, col_blocks):
    slots, block, _ = values.shape
    chunks = 8
    in_hbm = [
        pltpu.with_memory_space_constraint(array, pltpu.HBM)
        for array in (rows, cols, values)
    ]
    return pl.pallas_call(
        functools.partial(densify_kernel, chunks, row_blocks, col_blocks),
        in_specs=[WHOLE] + [pl.BlockSpec(memory_space=pltpu.HBM)] * 3,
        out_specs=WHOLE,
        out_shape=jax.ShapeDtypeStruct((row_blocks * block, col_blocks * block), BF16),
        scratch_shapes=[
            pltpu.VMEM(values.shape, BF16),
            pltpu.VMEM((row_blocks * col_blocks, block, block), F32),
            pltpu.SMEM((1, 1), jnp.int32),
            pltpu.SMEM(rows.shape, jnp.int32),
            pltpu.SMEM(cols.shape, jnp.int32),
            pltpu.SemaphoreType.DMA((chunks,)),
            pltpu.SemaphoreType.DMA((3,)),
        ],
        compiler_params=LIMIT,
        cost_estimate=pl.CostEstimate(flops=slots * block * block, bytes_accessed=values.size * 2, transcendentals=0),
        name="densify",
    )(count.reshape(1, 1), *in_hbm)


def forward_kernel(mine, tile_ref, outer_ref, x1, x2, out_ref):
    row = lax.axis_index("row")
    core = lax.rem(lax.axis_index("col"), 2)
    half = core if mine else 1 - core
    rows = x1.shape[0]
    for x in range(2):
        row_at = pl.multiple_of((2 * x + half) * rows, rows)
        total = None
        for k, shard in ((0, outer_ref[:rows, :]), (3, outer_ref[rows:, :]), (1, x1[...]), (2, x2[...])):
            col_at = pl.multiple_of(jnp.bitwise_xor(row, k) * rows, rows)
            tile = tile_ref[pl.ds(row_at, rows), pl.ds(col_at, rows)]
            term = jnp.dot(tile, shard, preferred_element_type=F32)
            total = term if total is None else total + term
        out_ref[pl.ds(x * rows, rows), :] = total.astype(out_ref.dtype)


def forward(mine, tile, outer, shards):
    rows, width_in = shards[0].shape
    return pl.pallas_call(
        functools.partial(forward_kernel, mine),
        in_specs=[WHOLE] * 4,
        out_specs=WHOLE,
        out_shape=jax.ShapeDtypeStruct((2 * rows, width_in), F32 if mine else BF16),
        compiler_params=LIMIT,
        cost_estimate=pl.CostEstimate(flops=tile.size * width_in, bytes_accessed=tile.size, transcendentals=0),
        name="forward_mine" if mine else "forward_sibling",
    )(tile, outer, *shards)


def layer_kernel(near_ref, far_ref, cot_ref, cot_far_ref, weight_ref, bias_ref, act_ref, swap_ref):
    mine = lax.rem(lax.axis_index("col") // 2, 2)
    rows, hid = cot_ref.shape
    width_in = near_ref.shape[1]
    weight = weight_ref[...]
    gw = None
    gb = None
    for other, source_ref in enumerate((cot_ref, cot_far_ref)):
        block = pl.ds(pl.multiple_of(jnp.bitwise_xor(mine, other) * rows, rows), rows)
        aggregate = (near_ref[block, :].astype(F32) + far_ref[block, :].astype(F32)).astype(BF16)
        pre_act = jnp.dot(aggregate, weight, preferred_element_type=F32) + bias_ref[...]
        sigmoid_pre = jax.nn.sigmoid(pre_act)
        if other == 0:
            act_ref[...] = pre_act
        cot = source_ref[...].astype(F32)
        pre_grad = (cot * sigmoid_pre * (1.0 + pre_act * (1.0 - sigmoid_pre))).astype(BF16)
        swap_ref[block, :] = lax.dot_general(
            pre_grad, weight, (((1,), (1,)), ((), ())), preferred_element_type=F32
        ).astype(BF16)
        term = lax.dot_general(
            aggregate, pre_grad, (((0,), (0,)), ((), ())), preferred_element_type=F32
        )
        bias_term = jnp.sum(pre_grad.astype(F32), axis=0, keepdims=True)
        gw = term if gw is None else gw + term
        gb = bias_term if gb is None else gb + bias_term
    at = 2 * rows
    for j in range(hid // width_in):
        lanes = slice(j * width_in, (j + 1) * width_in)
        swap_ref[pl.ds(at + j * width_in, width_in), :] = gw[:, lanes].astype(BF16)
    at = at + hid
    swap_ref[pl.ds(at, BIAS_ROWS), :] = jnp.concatenate(
        [gb[:, j * width_in : (j + 1) * width_in] for j in range(hid // width_in)]
        + [jnp.zeros((BIAS_ROWS - hid // width_in, width_in), F32)],
        axis=0,
    ).astype(BF16)


def backward_terms(tile_ref, half, k, grad_ref, rows):
    col_at = pl.multiple_of(jnp.bitwise_xor(lax.axis_index("row"), k) * rows, rows)
    total = None
    for x in range(2):
        row_at = pl.multiple_of((2 * x + half) * rows, rows)
        term = lax.dot_general(
            tile_ref[pl.ds(row_at, rows), pl.ds(col_at, rows)],
            grad_ref[pl.ds(x * rows, rows), :],
            (((0,), (0,)), ((), ())),
            preferred_element_type=F32,
        )
        total = term if total is None else total + term
    return total


def backward_mine_kernel(tile_ref, own_ref, part_ref):
    core = lax.rem(lax.axis_index("col"), 2)
    for k in range(ROWS):
        part_ref[k] = backward_terms(tile_ref, core, k, own_ref, part_ref.shape[1])


def turn_kernel(tile_ref, turned_ref):
    core = lax.rem(lax.axis_index("col"), 2)
    width = turned_ref.shape[1] // 2
    for x in range(2):
        row_at = pl.multiple_of((2 * x + 1 - core) * width, width)
        for c in range(turned_ref.shape[0] // width):
            lanes = slice(c * width, (c + 1) * width)
            turned_ref[lanes, x * width : (x + 1) * width] = tile_ref[pl.ds(row_at, width), lanes].T


def backward_kernel(turned_ref, sib_ref, part_ref, keep_ref, send1, send2, send3):
    row = lax.axis_index("row")
    rows = keep_ref.shape[0]
    for k, out in ((1, send1), (2, send2), (3, send3), (0, keep_ref)):
        at = pl.multiple_of(jnp.bitwise_xor(row, k) * rows, rows)
        total = part_ref[k] + jnp.dot(
            turned_ref[pl.ds(at, rows), :], sib_ref[pl.ds(0, 2 * rows), :], preferred_element_type=F32
        )
        out[...] = total.astype(out.dtype)


def stripe_kernel(own_ref, sib_ref, stripe_ref):
    core = lax.rem(lax.axis_index("col"), 2)
    width_in = own_ref.shape[1]
    first = own_ref.shape[0] - BIAS_ROWS - 2 * width_in
    for source, target, size in (
        (pl.multiple_of(first + core * width_in, BIAS_ROWS), 0, width_in),
        (own_ref.shape[0] - BIAS_ROWS, width_in, BIAS_ROWS),
    ):
        stripe_ref[pl.ds(target, size), :] = (
            own_ref[pl.ds(source, size), :].astype(F32) + sib_ref[pl.ds(source, size), :].astype(F32)
        ).astype(BF16)


def last_kernel(scale, keep_ref, got3, act_ref, pair_ref, pair_far_ref, half_ref, sib_ref,
                features_ref, hidden_ref, gw_ref, gb_ref):
    core = lax.rem(lax.axis_index("col"), 2)
    width_in, hid = gw_ref.shape
    half = half_ref[...] * scale
    sib = sib_ref[...] * scale
    for j in range(2):
        gw_ref[:, j * width_in : (j + 1) * width_in] = jnp.where(core == j, half, sib)
    block = pl.ds(width_in, BIAS_ROWS)
    both = (pair_ref[block, :].astype(F32) + pair_far_ref[block, :].astype(F32)) * scale
    for j in range(hid // width_in):
        gb_ref[:, j * width_in : (j + 1) * width_in] = both[j : j + 1, :]
    features_ref[...] = (keep_ref[...] + got3[...].astype(F32)).astype(BF16)
    hidden_ref[...] = act_ref[...]


def swap(array, axis, bit):
    size = lax.axis_size(axis)
    return lax.ppermute(array, axis, [(i, i ^ bit) for i in range(size)])


def dense_tile(features, block_values, block_rows, block_cols, block_count, weight, bias, cotangent):
    block_size = block_values.shape[1]
    node_rows = cotangent.shape[0]
    width_in = features.shape[1]
    hid = cotangent.shape[1]
    row_blocks = COLS * node_rows // block_size
    col_blocks = ROWS * node_rows // block_size
    extra = hid + BIAS_ROWS
    shards = [swap(features, "row", k) for k in (1, 2)]
    outer = jnp.concatenate([features, swap(features, "row", 3)])
    tile = densify(block_values, block_rows, block_cols, block_count, row_blocks, col_blocks)
    cot_far = swap(cotangent, "col", 2)
    send = forward(False, tile, outer, shards)
    keep = forward(True, tile, outer, shards)
    sib, cot_far = lax.optimization_barrier((swap(send, "col", 1), cot_far))
    near = (keep + sib.astype(F32)).astype(BF16)
    near, tile = lax.optimization_barrier((near, tile))
    turned = pl.pallas_call(
        turn_kernel,
        in_specs=[WHOLE],
        out_specs=WHOLE,
        out_shape=jax.ShapeDtypeStruct((ROWS * node_rows, 2 * node_rows), BF16),
        compiler_params=LIMIT,
        name="turn",
    )(tile)
    far, turned = lax.optimization_barrier((swap(near, "col", 2), turned))
    pre_act, grads = pl.pallas_call(
        layer_kernel,
        in_specs=[WHOLE] * 6,
        out_specs=[WHOLE] * 2,
        out_shape=[
            pltpu.VMEM((node_rows, hid), F32),
            jax.ShapeDtypeStruct((2 * node_rows + extra, width_in), BF16),
        ],
        compiler_params=LIMIT,
        name="layer",
    )(near, far, cotangent, cot_far, weight, bias.reshape(1, hid))
    block = jax.ShapeDtypeStruct((node_rows, width_in), BF16)
    part = pl.pallas_call(
        backward_mine_kernel,
        in_specs=[WHOLE] * 2,
        out_specs=WHOLE,
        out_shape=jax.ShapeDtypeStruct((ROWS, node_rows, width_in), F32),
        compiler_params=LIMIT,
        cost_estimate=pl.CostEstimate(flops=tile.size * width_in, bytes_accessed=tile.size, transcendentals=0),
        name="backward_mine",
    )(tile, grads)
    part, grads_sib = lax.optimization_barrier((part, swap(grads, "col", 1)))
    stripe = pl.pallas_call(
        stripe_kernel,
        in_specs=[WHOLE] * 2,
        out_specs=WHOLE,
        out_shape=jax.ShapeDtypeStruct((width_in + BIAS_ROWS, width_in), BF16),
        compiler_params=LIMIT,
        name="stripe",
    )(grads, grads_sib)
    stripe_far = swap(stripe, "row", 2)
    own, *sends = pl.pallas_call(
        backward_kernel,
        in_specs=[WHOLE] * 3,
        out_specs=[WHOLE] * 4,
        out_shape=[jax.ShapeDtypeStruct(block.shape, F32)] + [block] * 3,
        compiler_params=LIMIT,
        name="backward",
    )(turned, grads_sib, part)
    pair = (stripe.astype(F32) + stripe_far.astype(F32)).astype(BF16)
    pair, sends[2] = lax.optimization_barrier((pair, sends[2]))
    got = [swap(send, "row", k) for k, send in zip((1, 2, 3), sends)]
    pair, pre_act = lax.optimization_barrier((pair, pre_act))
    hidden = (pre_act * jax.nn.sigmoid(pre_act)).astype(BF16)
    pair_far = swap(pair, "row", 1)
    gw_half = pair[:width_in].astype(F32) + pair_far[:width_in].astype(F32)
    gw_half, hidden = lax.optimization_barrier((gw_half, hidden))
    gw_sib = swap(gw_half, "col", 1)
    norm_scale = float(node_rows * ROWS * COLS) ** (-0.5)
    grad_features, hidden, grad_weight, grad_bias = pl.pallas_call(
        functools.partial(last_kernel, norm_scale),
        in_specs=[WHOLE] * 7,
        out_specs=[WHOLE] * 4,
        out_shape=[
            block,
            jax.ShapeDtypeStruct(hidden.shape, BF16),
            jax.ShapeDtypeStruct((width_in, hid), F32),
            jax.ShapeDtypeStruct((1, hid), F32),
        ],
        compiler_params=LIMIT,
        name="last",
    )(own + got[0].astype(F32) + got[1].astype(F32), got[2], hidden, pair, pair_far, gw_half, gw_sib)
    return hidden, grad_weight, grad_bias.reshape(hid), grad_features


def solution(mesh):
    in_specs = (
        P(("parts", "col", "row"), None),
        P(("parts", "row", "col"), None, None),
        P(("parts", "row", "col")),
        P(("parts", "row", "col")),
        P(("parts", "row", "col")),
        P(),
        P(),
        P(("parts", "row", "col"), None),
    )
    out_specs = (
        P(("parts", "row", "col"), None),
        P("parts", None),
        P("parts"),
        P(("parts", "col", "row"), None),
    )
    small = mesh.shape["row"] == ROWS and mesh.shape["col"] == COLS
    return jax.shard_map(
        dense_tile if small else by_slots,
        mesh=mesh,
        in_specs=in_specs,
        out_specs=out_specs,
        check_vma=False,
    )
```
